256 devices in a mesh: row: 64 (over z, x, y_hi), col: 4 (over y_lo, core).
Axes of the slice: x: 4, y: 4 (y_hi: 2, y_lo: 2; y = y_hi * 2 + y_lo), z: 8, core: 2. Of those that a mesh axis runs over, the one named last changes fastest.
Arguments:
- panel: bfloat16 [524288, 256], P(('row', 'col')), may hold values from 0 to 2
- source: bfloat16 [524288, 256], P(('row', 'col')), may hold values from 0 to 2
- reflect: float32 [524288], P(('row', 'col')), may hold values from 0.1 to 0.9
- blocks: bfloat16 [4096, 512, 512], P(('row', 'col')), may hold values from 0 to 0.001953125
- blk_rows: int32 [256, 16], P(('row', 'col')), may hold values from 0 to 1023, as said below
- blk_cols: int32 [256, 16], P(('row', 'col')), may hold values from 0 to 1023, as said below
- live_count: int32 [256], P(('row', 'col')), may hold values from 1 to 16, as said below
Outputs:
- radiosity: float32 [524288, 256], P(('row', 'col'))
The draws below stay inside these ranges and needn't reach their ends.
Inputs may be any that keep to these rules, and one draw needn't show every extreme that they name: `blk_rows`: every block row of device d lies in row group d // 4, the block rows d // 4 * 4 * 4 to that plus 4 * 4 - 1; pairs may repeat and then add. `blk_cols`: each block column is at least its slot's block row and lies in the same row group or the next one. `live_count`: some device has all 16 slots live in every draw.
All inputs are finite; a program needn't handle non-finite values.
Results may differ from the reference program's by a relative error of at most 0.0003.
Values may be sent and summed in bfloat16 or wider, within the bound.
No kernel may reach another device: no remote copies, remote signals or barrier semaphores. Data moves between devices by JAX's collectives and lax.ppermute only.
A program may use at most 128 MiB of HBM per device.

```python
import math
import jax
import jax.numpy as jnp
from jax import lax

BLK = 512
WIDTH = 256
PB_DEV = 4
NNZ_DEV = 16
NB = 1024
ZONES = 524288
N_COL = 4
DEVICES = 256


def pattern(key):
    key_rows, key_cols, key_live, key_full = jax.random.split(key, 4)
    group_blocks = PB_DEV * N_COL
    device_ids = jnp.arange(DEVICES, dtype=jnp.int32)[:, None]
    base = device_ids // N_COL * group_blocks
    offsets = jax.random.randint(key_rows, (DEVICES, NNZ_DEV), 0, group_blocks, dtype=jnp.int32)
    rows = base + offsets
    span_end = jnp.minimum(base + 2 * group_blocks, NB)
    avail = span_end - rows
    steps_up = jax.random.randint(key_cols, (DEVICES, NNZ_DEV), 0, 2 * group_blocks, dtype=jnp.int32)
    cols = rows + steps_up % avail
    rows = rows.at[0, 0].set(0)
    cols = cols.at[0, 0].set(0)
    rows = rows.at[DEVICES - 1, 0].set(NB - 1)
    cols = cols.at[DEVICES - 1, 0].set(NB - 1)
    values = jax.random.randint(key_live, (DEVICES,), 0, NNZ_DEV, dtype=jnp.int32)
    counts = 1 + values * values // NNZ_DEV
    counts = jnp.minimum(counts, NNZ_DEV)
    full_device = jax.random.randint(key_full, (), 0, DEVICES, dtype=jnp.int32)
    counts = counts.at[full_device].set(NNZ_DEV)
    return (rows, cols, counts)


def draw_blk_rows(key, part):
    return pattern(key)[0]


def draw_blk_cols(key, part):
    return pattern(key)[1]


def draw_live_count(key, part):
    return pattern(key)[2]


def level_of(key, dims, pieces, smallest, largest):
    def one(axis_at, shards_of):
        heights = jax.random.uniform(jax.random.fold_in(jax.random.fold_in(key, 6), axis_at), (shards_of,), jnp.float32, smallest / len(pieces), largest / len(pieces))
        return jnp.repeat(jnp.exp(heights), dims[axis_at] // shards_of).reshape((-1,) + (1,) * (len(dims) - axis_at - 1))

    loudness = one(*pieces[0])
    for cut in pieces[1:]:
        loudness = loudness * one(*cut)
    return loudness


def setup_inputs(seed: int = 0) -> dict:
    arg_keys = jax.random.split(jax.random.key(seed), 8)
    panel = jnp.clip(2.0 * jax.random.uniform(arg_keys[0], (ZONES, WIDTH), jnp.float32) ** level_of(arg_keys[0], (ZONES, WIDTH), ((0, 256),), -0.2, 0.2), 0.0, 2.0).astype(jnp.bfloat16)
    source = jnp.clip(2.0 * jax.random.uniform(arg_keys[1], (ZONES, WIDTH), jnp.float32) ** level_of(arg_keys[1], (ZONES, WIDTH), ((0, 256),), -0.2, 0.2), 0.0, 2.0).astype(jnp.bfloat16)
    reflect = jnp.clip(jnp.exp(math.log(0.9) - 2.1972245 * jax.random.uniform(arg_keys[2], (ZONES,), jnp.float32) ** level_of(arg_keys[2], (ZONES,), ((0, 256),), -0.2, 0.2)), 0.1, 0.9)
    blocks = jnp.clip(0.001953125 * jax.random.uniform(arg_keys[3], (DEVICES * NNZ_DEV, BLK, BLK), jnp.float32) ** level_of(arg_keys[3], (DEVICES * NNZ_DEV, BLK, BLK), ((0, 256),), -0.2, 0.2), 0.0, 0.001953125).astype(jnp.bfloat16)
    blk_rows = draw_blk_rows(jax.random.fold_in(arg_keys[7], 71), 0)
    blk_cols = draw_blk_cols(jax.random.fold_in(arg_keys[7], 71), 0)
    live_count = draw_live_count(jax.random.fold_in(arg_keys[7], 71), 0)
    return {"panel": panel, "source": source, "reflect": reflect, "blocks": blocks, "blk_rows": blk_rows, "blk_cols": blk_cols, "live_count": live_count}


def reference(panel, source, reflect, blocks, blk_rows, blk_cols, live_count):
    rows_flat = blk_rows.reshape(-1).astype(jnp.int32)
    cols_flat = blk_cols.reshape(-1).astype(jnp.int32)
    slot_ids = jnp.arange(NNZ_DEV, dtype=jnp.int32)[None, :]
    live_flat = (slot_ids < live_count[:, None]).reshape(-1)
    total = jnp.zeros((ZONES, WIDTH), jnp.float32)

    def step(total, item):
        block, row_blk, col_blk, live = item
        weight = jnp.where(live, 1.0, 0.0).astype(jnp.float32)
        start_row = (row_blk * BLK).astype(jnp.int32)
        start_col = (col_blk * BLK).astype(jnp.int32)
        from_col = lax.dynamic_slice_in_dim(panel, start_col, BLK, 0)
        from_row = lax.dynamic_slice_in_dim(panel, start_row, BLK, 0)
        direct = jnp.dot(block, from_col, preferred_element_type=jnp.float32) * weight
        mirror = lax.dot_general(block, from_row, (((0,), (0,)), ((), ())), preferred_element_type=jnp.float32) * weight
        current = lax.dynamic_slice_in_dim(total, start_row, BLK, 0)
        total = lax.dynamic_update_slice_in_dim(total, current + direct, start_row, 0)
        current = lax.dynamic_slice_in_dim(total, start_col, BLK, 0)
        total = lax.dynamic_update_slice_in_dim(total, current + mirror, start_col, 0)
        return total, None

    total, _ = lax.scan(step, total, (blocks, rows_flat, cols_flat, live_flat))
    return source.astype(jnp.float32) + reflect[:, None] * total
```

```python
import jax
import jax.numpy as jnp
from jax import lax
from jax.experimental import pallas as pl
from jax.experimental.pallas import tpu as pltpu
from jax.sharding import PartitionSpec as P


AXES = ("row", "col")
SCALE_ROWS = 16
STEPS = 32766.0
LOG_STEPS = 256.0
LN2 = 0.6931471805599453
VMEM = 56 * 1024 * 1024
PARAMS = pltpu.CompilerParams(vmem_limit_bytes=VMEM)


def send(x, route):
    groups, cols = lax.axis_size("row"), lax.axis_size("col")
    pairs = []
    for r in range(groups):
        for c in range(cols):
            to_r, to_h, to_k = route(r, c // 2, c % 2)
            pairs.append((r * cols + c, to_r % groups * cols + to_h * 2 + to_k))
    return lax.ppermute(x, AXES, pairs)


def quantized(x):
    top = jnp.max(jnp.abs(x), axis=0, keepdims=True)
    log = jnp.ceil(jnp.log(jnp.maximum(top, 1e-30)) * (LOG_STEPS / LN2))
    inverse = STEPS * jnp.exp(log * (-LN2 / LOG_STEPS))
    steps = jnp.round(x * inverse).astype(jnp.int32).astype(jnp.int16)
    return steps, log.astype(jnp.int32)


def store_quantized(ref, at, x):
    steps, log = quantized(x)
    blk, half = x.shape
    ref[at, :blk, :] = steps
    ref[at, blk:, :] = jnp.broadcast_to(log, (SCALE_ROWS, half)).astype(jnp.int16)


def load_quantized(ref, at, blk):
    log = ref[at, blk:, :].astype(jnp.int32).astype(jnp.float32)[:1]
    scale = jnp.exp(log * (LN2 / LOG_STEPS)) * (1.0 / STEPS)
    return ref[at, :blk, :].astype(jnp.int32).astype(jnp.float32) * scale


def split_columns(panel, k):
    half = panel.shape[1] // 2
    left, right = panel[:, :half], panel[:, half:]
    first = k == 0
    return jnp.where(first, left, right), jnp.where(first, right, left)


def slot_specs(per_step, steps, blk):
    def own(s, meta):
        return jnp.minimum(jnp.minimum(s, steps - 1), (meta[2, 0] - 1) // per_step), 0, 0

    def sibling(s, meta):
        return jnp.minimum(jnp.maximum(s - steps, 0), (meta[2, 1] - 1) // per_step), 0, 0

    shape = (per_step, blk, blk)
    return [pl.BlockSpec(shape, own), pl.BlockSpec(shape, sibling)]


def load_pieces(pieces, x, sems, pb):
    copies = [
        pltpu.make_async_copy(piece, x.at[pl.ds(i * pb, pb)], sems.at[i])
        for i, piece in enumerate(pieces)
    ]
    for copy in copies:
        copy.start()
    return copies


def for_live_slots(meta, blocks, sib_blocks, per_step, steps, body):
    s = pl.program_id(0)
    n_slots = per_step * steps

    def run(ref, first, live):
        for g in range(per_step):
            slot = first + g

            @pl.when(slot < live)
            def _():
                body(ref.at[g], slot)

    @pl.when(s < steps)
    def _():
        run(blocks, s * per_step, meta[2, 0])

    @pl.when(s >= steps)
    def _():
        run(sib_blocks, s * per_step, meta[2, 1] + n_slots)


def mirror_kernel(pb, per_step, steps, meta, blocks, sib_blocks, *refs):
    pieces = refs[:4]
    far0, far1, near0, near1, own, x, acc, sems = refs[4:]
    blk = blocks.shape[1]
    s = pl.program_id(0)

    @pl.when(s == 0)
    def _():
        copies = load_pieces(pieces, x, sems, pb)
        acc[...] = jnp.zeros_like(acc)
        own[...] = jnp.zeros_like(own)
        for copy in copies:
            copy.wait()

    def body(block, slot):
        row, col = meta[0, slot], meta[1, slot]
        product = lax.dot_general(
            block[...], x[row], (((0,), (0,)), ((), ())), preferred_element_type=jnp.float32
        )
        at = col % (4 * pb)

        @pl.when(col < 4 * pb)
        def _():
            own[at] += product

        @pl.when(col >= 4 * pb)
        def _():
            acc[at] += product

    for_live_slots(meta, blocks, sib_blocks, per_step, steps, body)

    @pl.when(s == 2 * steps - 1)
    def _():
        for b in range(pb):
            store_quantized(far0, b, acc[b])
            store_quantized(far1, b, acc[pb + b])
            near0[b] = acc[2 * pb + b]
            store_quantized(near1, b, acc[3 * pb + b])


def direct_kernel(pb, per_step, steps, meta, blocks, sib_blocks, *refs):
    pieces, mirrored = refs[:8], refs[8]
    own0, own1, other0, other1, x, acc, sems = refs[9:]
    s = pl.program_id(0)

    @pl.when(s == 0)
    def _():
        copies = load_pieces(pieces, x, sems, pb)
        copy = pltpu.make_async_copy(mirrored, acc, sems.at[8])
        copy.start()
        for c in copies + [copy]:
            c.wait()

    def body(block, slot):
        row, col = meta[0, slot], meta[1, slot]
        acc[row] += jnp.dot(block[...], x[col], preferred_element_type=jnp.float32)

    for_live_slots(meta, blocks, sib_blocks, per_step, steps, body)

    @pl.when(s == 2 * steps - 1)
    def _():
        for b in range(pb):
            own0[b] = acc[b]
            own1[b] = acc[pb + b]
            store_quantized(other0, b, acc[2 * pb + b])
            other1[b] = acc[3 * pb + b]


def add_kernel(mine, arrived, out):
    blk = mine.shape[1]
    store_quantized(out, 0, mine[0] + load_quantized(arrived, 0, blk))


def final_kernel(meta, own, sib, pair0, pair1, below0, below1, source, reflect, out):
    blk, half = own.shape[1:]
    mine = own[0] + load_quantized(pair0, 0, blk) + load_quantized(below0, 0, blk)
    other = sib[0] + load_quantized(pair1, 0, blk) + load_quantized(below1, 0, blk)
    first = meta[2, 2] == 0
    factor = reflect[...]
    left = jnp.where(first, mine, other)
    right = jnp.where(first, other, mine)
    out[:, :half] = source[:, :half].astype(jnp.float32) + factor * left
    out[:, half:] = source[:, half:].astype(jnp.float32) + factor * right


def per_device(panel, source, reflect, blocks, blk_rows, blk_cols, live_count):
    f32 = jnp.float32
    piece_rows, width = panel.shape
    n_slots, blk, _ = blocks.shape
    half = width // 2
    pb = piece_rows // blk
    group_blocks = pb * lax.axis_size("col")
    r, c = lax.axis_index("row"), lax.axis_index("col")
    k = c % 2

    index = jnp.concatenate([blk_rows[0], blk_cols[0], live_count])
    sib_index = send(index, lambda r, h, k: (r, h, 1 - k))
    both = jnp.stack([index, sib_index])
    rows = both[:, :n_slots].reshape(-1) - r * group_blocks
    cols = both[:, n_slots : 2 * n_slots].reshape(-1) - r * group_blocks
    turn = c * pb
    last = jnp.zeros((2 * n_slots,), jnp.int32)
    last = last.at[0].set(both[0, -1]).at[1].set(both[1, -1]).at[2].set(k)
    meta = jnp.stack([rows ^ turn, cols ^ turn, last])

    mine, other = split_columns(panel, k)
    sib_blocks = send(blocks, lambda r, h, k: (r, h, 1 - k))
    pair1 = send(other, lambda r, h, k: (r, 1 - h, 1 - k))
    pair0 = send(mine, lambda r, h, k: (r, 1 - h, k))
    near0 = send(mine, lambda r, h, k: (r - 1, 1 - h, k))
    near1 = send(other, lambda r, h, k: (r - 1, 1 - h, 1 - k))
    sib = send(other, lambda r, h, k: (r, h, 1 - k))
    far0 = send(near0, lambda r, h, k: (r, 1 - h, k))
    far1 = send(pair1, lambda r, h, k: (r - 1, 1 - h, k))

    factor = jnp.broadcast_to(reflect[:, None], (piece_rows, half))
    as_blocks = lambda x: x.reshape(pb, blk, half)
    own_panel = [as_blocks(x) for x in (mine, sib, pair0, pair1)]
    next_panel = [as_blocks(x) for x in (far0, far1, near0, near1)]

    per_step = 4
    steps = n_slots // per_step
    flops = 2 * n_slots * 2 * blk * blk * half
    any_space = pl.BlockSpec(memory_space=pl.ANY)
    whole = lambda shape: pl.BlockSpec(shape, lambda s, meta: (0,) * len(shape))
    sums = jax.ShapeDtypeStruct((pb, blk, half), f32)
    sent = jax.ShapeDtypeStruct((pb, blk + SCALE_ROWS, half), jnp.int16)
    group = jax.ShapeDtypeStruct((4 * pb, blk, half), f32)

    far_q0, far_q1, near_f0, near_q1, mirrored = pl.pallas_call(
        lambda *refs: mirror_kernel(pb, per_step, steps, *refs),
        grid_spec=pltpu.PrefetchScalarGridSpec(
            num_scalar_prefetch=1,
            grid=(2 * steps,),
            in_specs=slot_specs(per_step, steps, blk) + [any_space] * 4,
            out_specs=[whole(s.shape) for s in (sent, sent, sums, sent, group)],
            scratch_shapes=[
                pltpu.VMEM((4 * pb, blk, half), panel.dtype),
                pltpu.VMEM((4 * pb, blk, half), f32),
                pltpu.SemaphoreType.DMA((4,)),
            ],
        ),
        out_shape=[sent, sent, sums, sent, group],
        compiler_params=PARAMS,
        cost_estimate=pl.CostEstimate(flops=2 * flops, bytes_accessed=32 << 20, transcendentals=0),
        name="mirror",
    )(meta, blocks, sib_blocks, *own_panel)

    part1 = send(far_q1, lambda r, h, k: (r + 1, 1 - h, k))
    part0 = send(far_q0, lambda r, h, k: (r, 1 - h, k))
    below1 = send(near_q1, lambda r, h, k: (r + 1, 1 - h, 1 - k))

    own_f0, own_f1, other_q0, other_f1 = pl.pallas_call(
        lambda *refs: direct_kernel(pb, per_step, steps, *refs),
        grid_spec=pltpu.PrefetchScalarGridSpec(
            num_scalar_prefetch=1,
            grid=(2 * steps,),
            in_specs=slot_specs(per_step, steps, blk) + [any_space] * 9,
            out_specs=[whole(s.shape) for s in (sums, sums, sent, sums)],
            scratch_shapes=[
                pltpu.VMEM((8 * pb, blk, half), panel.dtype),
                pltpu.VMEM((4 * pb, blk, half), f32),
                pltpu.SemaphoreType.DMA((9,)),
            ],
        ),
        out_shape=[sums, sums, sent, sums],
        compiler_params=PARAMS,
        cost_estimate=pl.CostEstimate(flops=2 * flops, bytes_accessed=32 << 20, transcendentals=0),
        name="direct",
    )(meta, blocks, sib_blocks, *own_panel, *next_panel, mirrored)

    def added(mine, arrived):
        one = lambda rows: pl.BlockSpec((1, rows, half), lambda i: (i, 0, 0))
        return pl.pallas_call(
            add_kernel,
            grid=(pb,),
            in_specs=[one(blk), one(blk + SCALE_ROWS)],
            out_specs=one(blk + SCALE_ROWS),
            out_shape=sent,
            compiler_params=PARAMS,
            cost_estimate=pl.CostEstimate(flops=1 << 20, bytes_accessed=2 << 20, transcendentals=0),
            name="added",
        )(mine, arrived)

    here0 = send(other_q0, lambda r, h, k: (r, 1 - h, k))
    here_sib = send(own_f1, lambda r, h, k: (r, h, 1 - k))
    below0 = send(added(near_f0, part0), lambda r, h, k: (r + 1, 1 - h, k))
    here1 = send(added(other_f1, part1), lambda r, h, k: (r, 1 - h, 1 - k))

    one = lambda rows: pl.BlockSpec((1, rows, half), lambda i, meta: (i, 0, 0))
    return pl.pallas_call(
        final_kernel,
        grid_spec=pltpu.PrefetchScalarGridSpec(
            num_scalar_prefetch=1,
            grid=(pb,),
            in_specs=[one(blk)] * 2
            + [one(blk + SCALE_ROWS)] * 4
            + [
                pl.BlockSpec((blk, width), lambda i, meta: (i, 0)),
                pl.BlockSpec((blk, half), lambda i, meta: (i, 0)),
            ],
            out_specs=pl.BlockSpec((blk, width), lambda i, meta: (i, 0)),
        ),
        out_shape=jax.ShapeDtypeStruct((piece_rows, width), f32),
        compiler_params=PARAMS,
        name="final",
    )(meta, own_f0, here_sib, here0, here1, below0, below1, source, factor)


def solution(mesh):
    return jax.shard_map(
        per_device,
        mesh=mesh,
        in_specs=(
            P(("row", "col"), None),
            P(("row", "col"), None),
            P(("row", "col")),
            P(("row", "col"), None, None),
            P(("row", "col"), None),
            P(("row", "col"), None),
            P(("row", "col")),
        ),
        out_specs=P(("row", "col"), None),
        check_vma=False,
    )
```

```python
import jax
import jax.numpy as jnp
from jax import lax
from jax.experimental import pallas as pl
from jax.experimental.pallas import tpu as pltpu
from jax.sharding import PartitionSpec as P


AXES = ("row", "col")
SCALE_ROWS = 16
STEPS = 32766.0
LOG_STEPS = 256.0
LN2 = 0.6931471805599453
PARAMS = pltpu.CompilerParams(vmem_limit_bytes=12 * 1024 * 1024)


def send(x, route):
    groups, cols = lax.axis_size("row"), lax.axis_size("col")
    pairs = []
    for r in range(groups):
        for c in range(cols):
            to_r, to_h, to_k = route(r, c // 2, c % 2)
            pairs.append((r * cols + c, to_r % groups * cols + to_h * 2 + to_k))
    return lax.ppermute(x, AXES, pairs)


def quantized(x):
    top = jnp.max(jnp.abs(x), axis=0, keepdims=True)
    log = jnp.ceil(jnp.log(jnp.maximum(top, 1e-30)) * (LOG_STEPS / LN2))
    inverse = STEPS * jnp.exp(log * (-LN2 / LOG_STEPS))
    steps = jnp.round(x * inverse).astype(jnp.int32).astype(jnp.int16)
    return steps, log.astype(jnp.int32)


def store_quantized(ref, at, x):
    steps, log = quantized(x)
    blk, half = x.shape
    ref[at, :blk, :] = steps
    ref[at, blk:, :] = jnp.broadcast_to(log, (SCALE_ROWS, half)).astype(jnp.int16)


def load_quantized(ref, at, blk):
    log = ref[at, blk:, :].astype(jnp.int32).astype(jnp.float32)[:1]
    scale = jnp.exp(log * (LN2 / LOG_STEPS)) * (1.0 / STEPS)
    return ref[at, :blk, :].astype(jnp.int32).astype(jnp.float32) * scale


def split_columns(panel, k):
    half = panel.shape[1] // 2
    left, right = panel[:, :half], panel[:, half:]
    first = k == 0
    return jnp.where(first, left, right), jnp.where(first, right, left)


def goes_on(earlier, sums):
    pass


def products(mirror, direct, index, sib_index, blocks, sib_blocks, pieces, sums, plan, ring, x, sems):
    n_slots, blk = blocks.shape[0], blocks.shape[1]
    group = sums.shape[0]
    pb, depth = group // 4, ring.shape[0]
    turn = index[2 * n_slots + 1] * pb
    none = len(pieces)

    def planned(n, pick):
        def scan(is_sib, table):
            def step(slot, n):
                hit, piece, b, at = pick(table[slot] ^ turn, table[n_slots + slot] ^ turn)
                plan[n] = (((at * pb + b) * 8 + piece) * 2 + is_sib) * n_slots + slot
                return n + jnp.where(hit, 1, 0)

            return step

        end = lax.fori_loop(0, index[2 * n_slots], scan(0, index), n)
        end = lax.fori_loop(0, sib_index[2 * n_slots], scan(1, sib_index), end)

        @pl.when((end - n) % 2 == 1)
        def _():
            last = plan[end - 1]
            plan[end] = last + (none - last // (2 * n_slots) % 8) * (2 * n_slots)

        return end + (end - n) % 2

    def pick_mirror(row, col):
        hit, first = mirror(row // (2 * pb), col // group)
        return hit, first + row // pb % 2, row % pb, col % group

    def pick_direct(row, col):
        hit, first = direct(col // (2 * pb))
        return hit, first + col // pb % 2, col % pb, row

    zero = jnp.int32(0)
    n_mirror = planned(zero, pick_mirror) if mirror else zero
    n = planned(n_mirror, pick_direct) if direct else n_mirror

    def copy(source, slot, i):
        at = i % depth
        return pltpu.make_async_copy(source.at[slot], ring.at[at], sems.at[at])

    def start(i):
        @pl.when(i < n)
        def _():
            entry = plan[i]
            slot, is_sib = entry % n_slots, entry // n_slots % 2

            @pl.when(is_sib == 0)
            def _():
                copy(blocks, slot, i).start()

            @pl.when(is_sib == 1)
            def _():
                copy(sib_blocks, slot, i).start()

    for i in range(depth):
        start(i)

    def staged(i, u):
        entry = plan[i] // (2 * n_slots)
        piece, b, at = entry % 8, entry // 8 % pb, entry // (8 * pb)
        for p, ref in enumerate(pieces):

            @pl.when(piece == p)
            def _():
                x[u] = ref[pl.ds(pl.multiple_of(b * blk, blk), blk), :]

        @pl.when(piece == none)
        def _():
            x[u] = jnp.zeros(x.shape[1:], x.dtype)

        return at

    def steps(first, end, product):
        def step(pair, carry):
            i = first + 2 * pair
            places = [staged(i + u, u) for u in range(2)]
            for u in range(2):
                copy(blocks, 0, i + u).wait()
            results = [product(ring[(i + u) % depth], x[u]) for u in range(2)]
            for at, result in zip(places, results):
                sums[at] += result
            for u in range(2):
                start(i + u + depth)
            return carry

        lax.fori_loop(0, (end - first) // 2, step, 0)

    if mirror:
        steps(
            zero,
            n_mirror,
            lambda block, x: lax.dot_general(
                block, x, (((0,), (0,)), ((), ())), preferred_element_type=jnp.float32
            ),
        )
    if direct:
        steps(
            n_mirror, n, lambda block, x: jnp.dot(block, x, preferred_element_type=jnp.float32)
        )


def for_blocks(pb, body):
    def step(b, carry):
        body(b)
        return carry

    lax.fori_loop(0, pb, step, 0)


def to_next(pair):
    return lambda rows, ahead: ((rows == pair) & (ahead == 1), 0)


def to_own(pair):
    return lambda rows, ahead: ((rows == pair) & (ahead == 0), 0)


def from_pair(pair):
    return lambda cols: (cols == pair, 0)


def chip_up_kernel(*refs):
    tables, pieces, sums, scratch = refs[:4], refs[4:6], refs[6], refs[7:]
    sums[...] = jnp.zeros_like(sums)
    products(to_next(0), None, *tables, pieces, sums, *scratch)


def chip_here_kernel(*refs):
    tables, pieces, sums, scratch = refs[:4], refs[4:6], refs[6], refs[7:]
    sums[...] = jnp.zeros_like(sums)
    products(to_own(0), from_pair(0), *tables, pieces, sums, *scratch)


def up_kernel(*refs):
    tables, pieces, earlier = refs[:4], refs[4:6], refs[6]
    far0, far1, near1, sums = refs[7:11]
    goes_on(earlier, sums)
    products(to_next(1), None, *tables, pieces, sums, *refs[11:])
    pb = far0.shape[0]

    def finish(b):
        store_quantized(far1, b, sums[pb + b])
        store_quantized(far0, b, sums[b])
        store_quantized(near1, b, sums[3 * pb + b])

    for_blocks(pb, finish)


def group_kernel(*refs):
    tables, pieces, earlier, sums = refs[:4], refs[4:8], refs[8], refs[9]
    goes_on(earlier, sums)
    direct = lambda cols: ((cols == 1) | (cols == 3), jnp.where(cols == 3, 2, 0))
    products(to_own(1), direct, *tables, pieces, sums, *refs[10:])


def far_kernel(*refs):
    tables, pieces, earlier = refs[:4], refs[4:6], refs[6]
    own1, other0, sums = refs[7:10]
    goes_on(earlier, sums)
    products(None, from_pair(2), *tables, pieces, sums, *refs[10:])
    pb = own1.shape[0]

    def finish(b):
        store_quantized(other0, b, sums[2 * pb + b])
        own1[b] = sums[pb + b]

    for_blocks(pb, finish)


def add_kernel(first, sums, arrived, out):
    blk = sums.shape[1]

    def step(b):
        store_quantized(out, b, sums[first + b] + load_quantized(arrived, b, blk))

    for_blocks(out.shape[0], step)


def final_kernel(index, sums, sib, pair0, pair1, below0, below1, source, reflect, out):
    blk, half = sums.shape[1:]
    b = pl.program_id(0)
    mine = sums[b] + load_quantized(pair0, b, blk) + load_quantized(below0, b, blk)
    other = sib[b] + load_quantized(pair1, b, blk) + load_quantized(below1, b, blk)
    first = index[index.shape[0] - 1] % 2 == 0
    rows = pl.ds(pl.multiple_of(b * blk, blk), blk)
    factor = reflect[rows, :]
    left = jnp.where(first, mine, other)
    right = jnp.where(first, other, mine)
    out[:, :half] = source[rows, :half].astype(jnp.float32) + factor * left
    out[:, half:] = source[rows, half:].astype(jnp.float32) + factor * right


def in_vmem(x):
    return pltpu.with_memory_space_constraint(x, pltpu.VMEM)


def in_hbm(x):
    return pltpu.with_memory_space_constraint(x, pltpu.HBM)


def vmem_shape(shape, dtype):
    return pltpu.VMEM(shape, dtype)


def call(kernel, name, inputs, outputs, aliases=None, scratch=()):
    def spec(shape, dtype):
        if dtype == jnp.int32:
            return pl.BlockSpec(memory_space=pltpu.SMEM)
        if shape[-1] > 128 and len(shape) == 3:
            return pl.BlockSpec(memory_space=pltpu.HBM)
        return pl.BlockSpec(memory_space=pltpu.VMEM)

    specs = [spec(x.shape, x.dtype) for x in inputs]
    put = {pltpu.VMEM: in_vmem, pltpu.HBM: in_hbm, pltpu.SMEM: lambda x: x}
    return pl.pallas_call(
        kernel,
        in_specs=specs,
        out_specs=[pl.BlockSpec(memory_space=pltpu.VMEM)] * len(outputs),
        out_shape=[vmem_shape(*output) for output in outputs],
        scratch_shapes=scratch,
        input_output_aliases=aliases or {},
        compiler_params=PARAMS,
        cost_estimate=pl.CostEstimate(flops=1000, bytes_accessed=1000, transcendentals=0),
        name=name,
    )(*[put[s.memory_space](x) for x, s in zip(inputs, specs)])


def per_device(panel, source, reflect, blocks, blk_rows, blk_cols, live_count):
    f32 = jnp.float32
    piece_rows, width = panel.shape
    n_slots, blk, _ = blocks.shape
    half = width // 2
    pb = piece_rows // blk
    r, c = lax.axis_index("row"), lax.axis_index("col")
    k = c % 2

    base = r * (pb * lax.axis_size("col"))
    place = c.astype(jnp.int32)[None]
    index = jnp.concatenate([blk_rows[0] - base, blk_cols[0] - base, live_count, place])

    to_sibling = lambda r, h, k: (r, h, 1 - k)
    across = lambda r, h, k: (r, 1 - h, k)
    down = lambda r, h, k: (r - 1, 1 - h, k)
    pair = send(panel, across)
    near = send(panel, down)
    sib_blocks = send(blocks, to_sibling)
    mine, other = split_columns(panel, k)
    sib = send(other, to_sibling)
    sib_index = send(index, to_sibling)
    sums = ((pb, blk, half), f32)
    sent = ((pb, blk + SCALE_ROWS, half), jnp.int16)
    group = ((4 * pb, blk, half), f32)
    tables = [index, sib_index, blocks, sib_blocks]
    scratch = [
        pltpu.SMEM((4 * n_slots + 4,), jnp.int32),
        pltpu.VMEM((6, blk, blk), blocks.dtype),
        pltpu.VMEM((2, blk, half), panel.dtype),
        pltpu.SemaphoreType.DMA((6,)),
    ]

    (up,) = call(chip_up_kernel, "chip_up", tables + [mine, sib], [group], scratch=scratch)
    pair, near, up = lax.optimization_barrier((pair, near, up))
    pair0, other = split_columns(pair, k)
    pair1 = send(other, to_sibling)
    near0, other = split_columns(near, k)
    near1 = send(other, to_sibling)
    far0 = send(near0, across)
    far1 = send(pair1, down)

    (here,) = call(chip_here_kernel, "chip_here", tables + [mine, sib], [group], scratch=scratch)
    up, here, near1 = lax.optimization_barrier((up, here, near1))
    far_q0, far_q1, near_q1, up = call(
        up_kernel, "up", tables + [pair0, pair1, up], [sent, sent, sent, group], {6: 3}, scratch
    )
    part1 = send(far_q1, lambda r, h, k: (r + 1, 1 - h, k))
    part0 = send(far_q0, across)
    below1 = send(near_q1, lambda r, h, k: (r + 1, 1 - h, 1 - k))

    (here,) = call(
        group_kernel, "group", tables + [pair0, pair1, near0, near1, here], [group], {8: 0}, scratch
    )
    far0, far1, here = lax.optimization_barrier((far0, far1, here))
    own_f1, other_q0, here = call(
        far_kernel, "far", tables + [far0, far1, here], [sums, sent, group], {6: 2}, scratch
    )
    here0 = send(other_q0, lambda r, h, k: (r, 1 - h, k))
    here_sib = send(own_f1, lambda r, h, k: (r, h, 1 - k))
    (below0,) = call(lambda *refs: add_kernel(2 * pb, *refs), "add_up", [up, part0], [sent])
    below0 = send(below0, lambda r, h, k: (r + 1, 1 - h, k))
    part1, below1 = lax.optimization_barrier((part1, below1))
    (here1,) = call(lambda *refs: add_kernel(3 * pb, *refs), "add_here", [here, part1], [sent])
    here1 = send(here1, lambda r, h, k: (r, 1 - h, 1 - k))

    factor = jnp.broadcast_to(reflect[:, None], (piece_rows, half))
    args = [here, here_sib, here0, here1, below0, below1, source, factor]
    return pl.pallas_call(
        final_kernel,
        grid=(pb,),
        in_specs=[pl.BlockSpec(memory_space=pltpu.SMEM)]
        + [pl.BlockSpec(memory_space=pltpu.VMEM)] * len(args),
        out_specs=pl.BlockSpec((blk, width), lambda i: (i, 0)),
        out_shape=jax.ShapeDtypeStruct((piece_rows, width), f32),
        compiler_params=PARAMS,
        name="final",
    )(index, *map(in_vmem, args))


def solution(mesh):
    return jax.shard_map(
        per_device,
        mesh=mesh,
        in_specs=(
            P(("row", "col"), None),
            P(("row", "col"), None),
            P(("row", "col")),
            P(("row", "col"), None, None),
            P(("row", "col"), None),
            P(("row", "col"), None),
            P(("row", "col")),
        ),
        out_specs=P(("row", "col"), None),
        check_vma=False,
    )
```

```python
import jax
import jax.numpy as jnp
from jax import lax
from jax.experimental import pallas as pl
from jax.experimental.pallas import tpu as pltpu
from jax.sharding import PartitionSpec as P


AXES = ("row", "col")
SCALE_ROWS = 16
STEPS = 32766.0
LOG_STEPS = 256.0
LN2 = 0.6931471805599453
PARAMS = pltpu.CompilerParams(vmem_limit_bytes=12 * 1024 * 1024)


def send(x, route):
    groups, cols = lax.axis_size("row"), lax.axis_size("col")
    pairs = []
    for r in range(groups):
        for c in range(cols):
            to_r, to_h, to_k = route(r, c // 2, c % 2)
            pairs.append((r * cols + c, to_r % groups * cols + to_h * 2 + to_k))
    return lax.ppermute(x, AXES, pairs)


def quantized(x):
    top = jnp.max(jnp.abs(x), axis=0, keepdims=True)
    log = jnp.ceil(jnp.log(jnp.maximum(top, 1e-30)) * (LOG_STEPS / LN2))
    inverse = STEPS * jnp.exp(log * (-LN2 / LOG_STEPS))
    steps = jnp.round(x * inverse).astype(jnp.int32).astype(jnp.int16)
    return steps, log.astype(jnp.int32)


def store_quantized(ref, at, x):
    steps, log = quantized(x)
    blk, half = x.shape
    ref[at, :blk, :] = steps
    ref[at, blk:, :] = jnp.broadcast_to(log, (SCALE_ROWS, half)).astype(jnp.int16)


def load_quantized(ref, at, blk):
    log = ref[at, blk:, :].astype(jnp.int32).astype(jnp.float32)[:1]
    scale = jnp.exp(log * (LN2 / LOG_STEPS)) * (1.0 / STEPS)
    return ref[at, :blk, :].astype(jnp.int32).astype(jnp.float32) * scale


def split_columns(panel, k):
    half = panel.shape[1] // 2
    left, right = panel[:, :half], panel[:, half:]
    first = k == 0
    return jnp.where(first, left, right), jnp.where(first, right, left)


def goes_on(earlier, sums):
    pass


def products(mirror, direct, index, sib_index, blocks, sib_blocks, pieces, sums, plan, ring, x, sems):
    n_slots, blk = blocks.shape[0], blocks.shape[1]
    group = sums.shape[0]
    pb, depth = group // 4, ring.shape[0]
    turn = index[2 * n_slots + 1] * pb
    none = len(pieces)

    def planned(n, pick):
        def scan(is_sib, table):
            def step(slot, n):
                hit, piece, b, at = pick(table[slot] ^ turn, table[n_slots + slot] ^ turn)
                plan[n] = (((at * pb + b) * 8 + piece) * 2 + is_sib) * n_slots + slot
                return n + jnp.where(hit, 1, 0)

            return step

        end = lax.fori_loop(0, index[2 * n_slots], scan(0, index), n)
        end = lax.fori_loop(0, sib_index[2 * n_slots], scan(1, sib_index), end)

        @pl.when((end - n) % 2 == 1)
        def _():
            last = plan[end - 1]
            plan[end] = last + (none - last // (2 * n_slots) % 8) * (2 * n_slots)

        return end + (end - n) % 2

    def pick_mirror(row, col):
        hit, first = mirror(row // (2 * pb), col // group)
        return hit, first + row // pb % 2, row % pb, col % group

    def pick_direct(row, col):
        hit, first = direct(col // (2 * pb))
        return hit, first + col // pb % 2, col % pb, row

    zero = jnp.int32(0)
    n_mirror = planned(zero, pick_mirror) if mirror else zero
    n = planned(n_mirror, pick_direct) if direct else n_mirror

    def copy(source, slot, i):
        at = i % depth
        return pltpu.make_async_copy(source.at[slot], ring.at[at], sems.at[at])

    def start(i):
        @pl.when(i < n)
        def _():
            entry = plan[i]
            slot, is_sib = entry % n_slots, entry // n_slots % 2

            @pl.when(is_sib == 0)
            def _():
                copy(blocks, slot, i).start()

            @pl.when(is_sib == 1)
            def _():
                copy(sib_blocks, slot, i).start()

    for i in range(depth):
        start(i)

    def staged(i, u):
        entry = plan[i] // (2 * n_slots)
        piece, b, at = entry % 8, entry // 8 % pb, entry // (8 * pb)
        for p, ref in enumerate(pieces):

            @pl.when(piece == p)
            def _():
                x[u] = ref[pl.ds(pl.multiple_of(b * blk, blk), blk), :]

        @pl.when(piece == none)
        def _():
            x[u] = jnp.zeros(x.shape[1:], x.dtype)

        return at

    def steps(first, end, product):
        def step(pair, carry):
            i = first + 2 * pair
            places = [staged(i + u, u) for u in range(2)]
            for u in range(2):
                copy(blocks, 0, i + u).wait()
            results = [product(ring[(i + u) % depth], x[u]) for u in range(2)]
            for at, result in zip(places, results):
                sums[at] += result
            for u in range(2):
                start(i + u + depth)
            return carry

        lax.fori_loop(0, (end - first) // 2, step, 0)

    if mirror:
        steps(
            zero,
            n_mirror,
            lambda block, x: lax.dot_general(
                block, x, (((0,), (0,)), ((), ())), preferred_element_type=jnp.float32
            ),
        )
    if direct:
        steps(
            n_mirror, n, lambda block, x: jnp.dot(block, x, preferred_element_type=jnp.float32)
        )


def for_blocks(pb, body):
    def step(b, carry):
        body(b)
        return carry

    lax.fori_loop(0, pb, step, 0)


def to_next(pair):
    return lambda rows, ahead: ((rows == pair) & (ahead == 1), 0)


def to_own(pair):
    return lambda rows, ahead: ((rows == pair) & (ahead == 0), 0)


def from_pair(pair):
    return lambda cols: (cols == pair, 0)


def chip_up_kernel(*refs):
    tables, pieces, sums, scratch = refs[:4], refs[4:6], refs[6], refs[7:]
    sums[...] = jnp.zeros_like(sums)
    products(to_next(0), None, *tables, pieces, sums, *scratch)


def chip_here_kernel(*refs):
    tables, pieces, sums, scratch = refs[:4], refs[4:6], refs[6], refs[7:]
    sums[...] = jnp.zeros_like(sums)
    products(to_own(0), from_pair(0), *tables, pieces, sums, *scratch)


def up_kernel(*refs):
    tables, pieces, earlier = refs[:4], refs[4:6], refs[6]
    far0, far1, near1, sums = refs[7:11]
    goes_on(earlier, sums)
    products(to_next(1), None, *tables, pieces, sums, *refs[11:])
    pb = far0.shape[0]

    def finish(b):
        store_quantized(far1, b, sums[pb + b])
        store_quantized(far0, b, sums[b])
        store_quantized(near1, b, sums[3 * pb + b])

    for_blocks(pb, finish)


def group_kernel(*refs):
    tables, pieces, earlier, sums = refs[:4], refs[4:8], refs[8], refs[9]
    goes_on(earlier, sums)
    direct = lambda cols: ((cols == 1) | (cols == 3), jnp.where(cols == 3, 2, 0))
    products(to_own(1), direct, *tables, pieces, sums, *refs[10:])


def far_kernel(*refs):
    tables, pieces, earlier = refs[:4], refs[4:6], refs[6]
    own1, other0, sums = refs[7:10]
    goes_on(earlier, sums)
    products(None, from_pair(2), *tables, pieces, sums, *refs[10:])
    pb = own1.shape[0]

    def finish(b):
        store_quantized(other0, b, sums[2 * pb + b])
        own1[b] = sums[pb + b]

    for_blocks(pb, finish)


def add_kernel(first, sums, arrived, out):
    blk = sums.shape[1]

    def step(b):
        store_quantized(out, b, sums[first + b] + load_quantized(arrived, b, blk))

    for_blocks(out.shape[0], step)


def final_kernel(index, sums, sib, pair0, pair1, below0, below1, source, reflect, out):
    blk, half = sums.shape[1:]
    b = pl.program_id(0)
    mine = sums[b] + load_quantized(pair0, b, blk) + load_quantized(below0, b, blk)
    other = sib[b] + load_quantized(pair1, b, blk) + load_quantized(below1, b, blk)
    first = index[index.shape[0] - 1] % 2 == 0
    rows = pl.ds(pl.multiple_of(b * blk, blk), blk)
    factor = reflect[rows, :]
    left = jnp.where(first, mine, other)
    right = jnp.where(first, other, mine)
    out[:, :half] = source[rows, :half].astype(jnp.float32) + factor * left
    out[:, half:] = source[rows, half:].astype(jnp.float32) + factor * right


def in_vmem(x):
    return pltpu.with_memory_space_constraint(x, pltpu.VMEM)


def in_hbm(x):
    return pltpu.with_memory_space_constraint(x, pltpu.HBM)


def vmem_shape(shape, dtype):
    return pltpu.VMEM(shape, dtype)


def call(kernel, name, inputs, outputs, aliases=None, scratch=()):
    def spec(shape, dtype):
        if dtype == jnp.int32:
            return pl.BlockSpec(memory_space=pltpu.SMEM)
        if shape[-1] > 128 and len(shape) == 3:
            return pl.BlockSpec(memory_space=pltpu.HBM)
        return pl.BlockSpec(memory_space=pltpu.VMEM)

    specs = [spec(x.shape, x.dtype) for x in inputs]
    put = {pltpu.VMEM: in_vmem, pltpu.HBM: in_hbm, pltpu.SMEM: lambda x: x}
    return pl.pallas_call(
        kernel,
        in_specs=specs,
        out_specs=[pl.BlockSpec(memory_space=pltpu.VMEM)] * len(outputs),
        out_shape=[vmem_shape(*output) for output in outputs],
        scratch_shapes=scratch,
        input_output_aliases=aliases or {},
        compiler_params=PARAMS,
        cost_estimate=pl.CostEstimate(flops=1000, bytes_accessed=1000, transcendentals=0),
        name=name,
    )(*[put[s.memory_space](x) for x, s in zip(inputs, specs)])


def per_device(panel, source, reflect, blocks, blk_rows, blk_cols, live_count):
    f32 = jnp.float32
    piece_rows, width = panel.shape
    n_slots, blk, _ = blocks.shape
    half = width // 2
    pb = piece_rows // blk
    r, c = lax.axis_index("row"), lax.axis_index("col")
    k = c % 2

    base = r * (pb * lax.axis_size("col"))
    place = c.astype(jnp.int32)[None]
    index = jnp.concatenate([blk_rows[0] - base, blk_cols[0] - base, live_count, place])

    to_sibling = lambda r, h, k: (r, h, 1 - k)
    across = lambda r, h, k: (r, 1 - h, k)
    down = lambda r, h, k: (r - 1, 1 - h, k)
    pair = send(panel, across)
    near = send(panel, down)
    sib_blocks = send(blocks, to_sibling)
    mine, other = split_columns(panel, k)
    sib = send(other, to_sibling)
    sib_index = send(index, to_sibling)
    sums = ((pb, blk, half), f32)
    sent = ((pb, blk + SCALE_ROWS, half), jnp.int16)
    group = ((4 * pb, blk, half), f32)
    tables = [index, sib_index, blocks, sib_blocks]
    scratch = [
        pltpu.SMEM((4 * n_slots + 4,), jnp.int32),
        pltpu.VMEM((6, blk, blk), blocks.dtype),
        pltpu.VMEM((2, blk, half), panel.dtype),
        pltpu.SemaphoreType.DMA((6,)),
    ]

    (up,) = call(chip_up_kernel, "chip_up", tables + [mine, sib], [group], scratch=scratch)
    (here,) = call(chip_here_kernel, "chip_here", tables + [mine, sib], [group], scratch=scratch)
    pair, up, here = lax.optimization_barrier((pair, up, here))
    pair0, other = split_columns(pair, k)
    near, _ = lax.optimization_barrier((near, other))
    far1 = send(other, lambda r, h, k: (r - 1, 1 - h, 1 - k))
    pair1 = send(other, to_sibling)
    near0, other = split_columns(near, k)
    near1 = send(other, to_sibling)
    far0 = send(near0, across)

    up, near1 = lax.optimization_barrier((up, near1))
    far_q0, far_q1, near_q1, up = call(
        up_kernel, "up", tables + [pair0, pair1, up], [sent, sent, sent, group], {6: 3}, scratch
    )
    part1 = send(far_q1, lambda r, h, k: (r + 1, 1 - h, k))
    part0 = send(far_q0, across)
    below1 = send(near_q1, lambda r, h, k: (r + 1, 1 - h, 1 - k))

    (here,) = call(
        group_kernel, "group", tables + [pair0, pair1, near0, near1, here], [group], {8: 0}, scratch
    )
    far0, far1, here = lax.optimization_barrier((far0, far1, here))
    own_f1, other_q0, here = call(
        far_kernel, "far", tables + [far0, far1, here], [sums, sent, group], {6: 2}, scratch
    )
    here0 = send(other_q0, lambda r, h, k: (r, 1 - h, k))
    here_sib = send(own_f1, lambda r, h, k: (r, h, 1 - k))
    (here1,) = call(lambda *refs: add_kernel(3 * pb, *refs), "add_here", [here, part1], [sent])
    part0, below1, _ = lax.optimization_barrier((part0, below1, here1))
    here1 = send(here1, lambda r, h, k: (r, 1 - h, 1 - k))
    (below0,) = call(lambda *refs: add_kernel(2 * pb, *refs), "add_up", [up, part0], [sent])
    below0 = send(below0, lambda r, h, k: (r + 1, 1 - h, k))

    factor = jnp.broadcast_to(reflect[:, None], (piece_rows, half))
    args = [here, here_sib, here0, here1, below0, below1, source, factor]
    return pl.pallas_call(
        final_kernel,
        grid=(pb,),
        in_specs=[pl.BlockSpec(memory_space=pltpu.SMEM)]
        + [pl.BlockSpec(memory_space=pltpu.VMEM)] * len(args),
        out_specs=pl.BlockSpec((blk, width), lambda i: (i, 0)),
        out_shape=jax.ShapeDtypeStruct((piece_rows, width), f32),
        compiler_params=PARAMS,
        name="final",
    )(index, *map(in_vmem, args))


def solution(mesh):
    return jax.shard_map(
        per_device,
        mesh=mesh,
        in_specs=(
            P(("row", "col"), None),
            P(("row", "col"), None),
            P(("row", "col")),
            P(("row", "col"), None, None),
            P(("row", "col"), None),
            P(("row", "col"), None),
            P(("row", "col")),
        ),
        out_specs=P(("row", "col"), None),
        check_vma=False,
    )
```

```python
import jax
import jax.numpy as jnp
from jax import lax
from jax.experimental import pallas as pl
from jax.experimental.pallas import tpu as pltpu
from jax.sharding import PartitionSpec as P


AXES = ("row", "col")
SCALE_ROWS = 16
STEPS = 32766.0
LOG_STEPS = 256.0
LN2 = 0.6931471805599453
PARAMS = pltpu.CompilerParams(vmem_limit_bytes=12 * 1024 * 1024)


def send(x, route):
    groups, cols = lax.axis_size("row"), lax.axis_size("col")
    pairs = []
    for r in range(groups):
        for c in range(cols):
            to_r, to_h, to_k = route(r, c // 2, c % 2)
            pairs.append((r * cols + c, to_r % groups * cols + to_h * 2 + to_k))
    return lax.ppermute(x, AXES, pairs)


def quantized(x):
    top = jnp.max(jnp.abs(x), axis=0, keepdims=True)
    log = jnp.ceil(jnp.log(jnp.maximum(top, 1e-30)) * (LOG_STEPS / LN2))
    inverse = STEPS * jnp.exp(log * (-LN2 / LOG_STEPS))
    steps = jnp.round(x * inverse).astype(jnp.int32).astype(jnp.int16)
    return steps, log.astype(jnp.int32)


def store_quantized(ref, at, x):
    steps, log = quantized(x)
    blk, half = x.shape
    ref[at, :blk, :] = steps
    ref[at, blk:, :] = jnp.broadcast_to(log, (SCALE_ROWS, half)).astype(jnp.int16)


def load_quantized(ref, at, blk):
    log = ref[at, blk:, :].astype(jnp.int32).astype(jnp.float32)[:1]
    scale = jnp.exp(log * (LN2 / LOG_STEPS)) * (1.0 / STEPS)
    return ref[at, :blk, :].astype(jnp.int32).astype(jnp.float32) * scale


def split_columns(panel, k):
    half = panel.shape[1] // 2
    left, right = panel[:, :half], panel[:, half:]
    first = k == 0
    return jnp.where(first, left, right), jnp.where(first, right, left)


def goes_on(earlier, sums):
    pass


def products(mirror, direct, index, sib_index, blocks, sib_blocks, pieces, sums, plan, ring, x, sems):
    n_slots, blk = blocks.shape[0], blocks.shape[1]
    group = sums.shape[0]
    pb, depth = group // 4, ring.shape[0]
    turn = index[2 * n_slots + 1] * pb
    none = len(pieces)

    def planned(n, pick):
        def scan(is_sib, table):
            def step(slot, n):
                hit, piece, b, at = pick(table[slot] ^ turn, table[n_slots + slot] ^ turn)
                plan[n] = (((at * pb + b) * 8 + piece) * 2 + is_sib) * n_slots + slot
                return n + jnp.where(hit, 1, 0)

            return step

        end = lax.fori_loop(0, index[2 * n_slots], scan(0, index), n)
        end = lax.fori_loop(0, sib_index[2 * n_slots], scan(1, sib_index), end)

        @pl.when((end - n) % 2 == 1)
        def _():
            last = plan[end - 1]
            plan[end] = last + (none - last // (2 * n_slots) % 8) * (2 * n_slots)

        return end + (end - n) % 2

    def pick_mirror(row, col):
        hit, first = mirror(row // (2 * pb), col // group)
        return hit, first + row // pb % 2, row % pb, col % group

    def pick_direct(row, col):
        hit, first = direct(col // (2 * pb))
        return hit, first + col // pb % 2, col % pb, row

    zero = jnp.int32(0)
    n_mirror = planned(zero, pick_mirror) if mirror else zero
    n = planned(n_mirror, pick_direct) if direct else n_mirror

    def copy(source, slot, i):
        at = i % depth
        return pltpu.make_async_copy(source.at[slot], ring.at[at], sems.at[at])

    def start(i):
        @pl.when(i < n)
        def _():
            entry = plan[i]
            slot, is_sib = entry % n_slots, entry // n_slots % 2

            @pl.when(is_sib == 0)
            def _():
                copy(blocks, slot, i).start()

            @pl.when(is_sib == 1)
            def _():
                copy(sib_blocks, slot, i).start()

    for i in range(depth):
        start(i)

    def staged(i, u):
        entry = plan[i] // (2 * n_slots)
        piece, b, at = entry % 8, entry // 8 % pb, entry // (8 * pb)
        for p, ref in enumerate(pieces):

            @pl.when(piece == p)
            def _():
                x[u] = ref[pl.ds(pl.multiple_of(b * blk, blk), blk), :]

        @pl.when(piece == none)
        def _():
            x[u] = jnp.zeros(x.shape[1:], x.dtype)

        return at

    def steps(first, end, product):
        def step(pair, carry):
            i = first + 2 * pair
            places = [staged(i + u, u) for u in range(2)]
            for u in range(2):
                copy(blocks, 0, i + u).wait()
            results = [product(ring[(i + u) % depth], x[u]) for u in range(2)]
            for at, result in zip(places, results):
                sums[at] += result
            for u in range(2):
                start(i + u + depth)
            return carry

        lax.fori_loop(0, (end - first) // 2, step, 0)

    if mirror:
        steps(
            zero,
            n_mirror,
            lambda block, x: lax.dot_general(
                block, x, (((0,), (0,)), ((), ())), preferred_element_type=jnp.float32
            ),
        )
    if direct:
        steps(
            n_mirror, n, lambda block, x: jnp.dot(block, x, preferred_element_type=jnp.float32)
        )


def for_blocks(pb, body):
    def step(b, carry):
        body(b)
        return carry

    lax.fori_loop(0, pb, step, 0)


def to_next(pair):
    return lambda rows, ahead: ((rows == pair) & (ahead == 1), 0)


def to_own(pair):
    return lambda rows, ahead: ((rows == pair) & (ahead == 0), 0)


def from_pair(pair):
    return lambda cols: (cols == pair, 0)


def chip_up_kernel(*refs):
    tables, pieces, sums, scratch = refs[:4], refs[4:6], refs[6], refs[7:]
    sums[...] = jnp.zeros_like(sums)
    products(to_next(0), None, *tables, pieces, sums, *scratch)


def chip_here_kernel(*refs):
    tables, pieces, sums, scratch = refs[:4], refs[4:6], refs[6], refs[7:]
    sums[...] = jnp.zeros_like(sums)
    products(to_own(0), from_pair(0), *tables, pieces, sums, *scratch)


def up_kernel(*refs):
    tables, pieces, earlier = refs[:4], refs[4:6], refs[6]
    far0, far1, near1, sums = refs[7:11]
    goes_on(earlier, sums)
    products(to_next(1), None, *tables, pieces, sums, *refs[11:])
    pb = far0.shape[0]

    def finish(b):
        store_quantized(far1, b, sums[pb + b])
        store_quantized(far0, b, sums[b])
        store_quantized(near1, b, sums[3 * pb + b])

    for_blocks(pb, finish)


def group_kernel(*refs):
    tables, pieces, earlier, sums = refs[:4], refs[4:8], refs[8], refs[9]
    goes_on(earlier, sums)
    direct = lambda cols: ((cols == 1) | (cols == 3), jnp.where(cols == 3, 2, 0))
    products(to_own(1), direct, *tables, pieces, sums, *refs[10:])


def far_kernel(*refs):
    tables, pieces, earlier = refs[:4], refs[4:6], refs[6]
    own1, other0, sums = refs[7:10]
    goes_on(earlier, sums)
    products(None, from_pair(2), *tables, pieces, sums, *refs[10:])
    pb = own1.shape[0]

    def finish(b):
        store_quantized(other0, b, sums[2 * pb + b])
        own1[b] = sums[pb + b]

    for_blocks(pb, finish)


def add_kernel(first, sums, arrived, out):
    blk = sums.shape[1]

    def step(b):
        store_quantized(out, b, sums[first + b] + load_quantized(arrived, b, blk))

    for_blocks(out.shape[0], step)


def final_kernel(index, sums, sib, pair0, pair1, below0, below1, source, reflect, out):
    blk, half = sums.shape[1:]
    b = pl.program_id(0)
    mine = sums[b] + load_quantized(pair0, b, blk) + load_quantized(below0, b, blk)
    other = sib[b] + load_quantized(pair1, b, blk) + load_quantized(below1, b, blk)
    first = index[index.shape[0] - 1] % 2 == 0
    rows = pl.ds(pl.multiple_of(b * blk, blk), blk)
    factor = reflect[rows, :]
    left = jnp.where(first, mine, other)
    right = jnp.where(first, other, mine)
    out[:, :half] = source[rows, :half].astype(jnp.float32) + factor * left
    out[:, half:] = source[rows, half:].astype(jnp.float32) + factor * right


def in_vmem(x):
    return pltpu.with_memory_space_constraint(x, pltpu.VMEM)


def in_hbm(x):
    return pltpu.with_memory_space_constraint(x, pltpu.HBM)


def vmem_shape(shape, dtype):
    return pltpu.VMEM(shape, dtype)


def call(kernel, name, inputs, outputs, aliases=None, scratch=()):
    def spec(shape, dtype):
        if dtype == jnp.int32:
            return pl.BlockSpec(memory_space=pltpu.SMEM)
        if shape[-1] > 128 and len(shape) == 3:
            return pl.BlockSpec(memory_space=pltpu.HBM)
        return pl.BlockSpec(memory_space=pltpu.VMEM)

    specs = [spec(x.shape, x.dtype) for x in inputs]
    put = {pltpu.VMEM: in_vmem, pltpu.HBM: in_hbm, pltpu.SMEM: lambda x: x}
    return pl.pallas_call(
        kernel,
        in_specs=specs,
        out_specs=[pl.BlockSpec(memory_space=pltpu.VMEM)] * len(outputs),
        out_shape=[vmem_shape(*output) for output in outputs],
        scratch_shapes=scratch,
        input_output_aliases=aliases or {},
        compiler_params=PARAMS,
        cost_estimate=pl.CostEstimate(flops=1000, bytes_accessed=1000, transcendentals=0),
        name=name,
    )(*[put[s.memory_space](x) for x, s in zip(inputs, specs)])


def per_device(panel, source, reflect, blocks, blk_rows, blk_cols, live_count):
    f32 = jnp.float32
    piece_rows, width = panel.shape
    n_slots, blk, _ = blocks.shape
    half = width // 2
    pb = piece_rows // blk
    r, c = lax.axis_index("row"), lax.axis_index("col")
    k = c % 2

    base = r * (pb * lax.axis_size("col"))
    place = c.astype(jnp.int32)[None]
    index = jnp.concatenate([blk_rows[0] - base, blk_cols[0] - base, live_count, place])

    to_sibling = lambda r, h, k: (r, h, 1 - k)
    across = lambda r, h, k: (r, 1 - h, k)
    down = lambda r, h, k: (r - 1, 1 - h, k)
    pair = send(panel, across)
    near = send(panel, down)
    sib_blocks = send(blocks, to_sibling)
    mine, other = split_columns(panel, k)
    sib = send(other, to_sibling)
    sib_index = send(index, to_sibling)
    sums = ((pb, blk, half), f32)
    sent = ((pb, blk + SCALE_ROWS, half), jnp.int16)
    group = ((4 * pb, blk, half), f32)
    tables = [index, sib_index, blocks, sib_blocks]
    scratch = [
        pltpu.SMEM((4 * n_slots + 4,), jnp.int32),
        pltpu.VMEM((6, blk, blk), blocks.dtype),
        pltpu.VMEM((2, blk, half), panel.dtype),
        pltpu.SemaphoreType.DMA((6,)),
    ]

    (up,) = call(chip_up_kernel, "chip_up", tables + [mine, sib], [group], scratch=scratch)
    (here,) = call(chip_here_kernel, "chip_here", tables + [mine, sib], [group], scratch=scratch)
    pair, up, here = lax.optimization_barrier((pair, up, here))
    pair0, other = split_columns(pair, k)
    near, _ = lax.optimization_barrier((near, other))
    far1 = send(other, lambda r, h, k: (r - 1, 1 - h, 1 - k))
    pair1 = send(other, to_sibling)
    near0, other = split_columns(near, k)
    near1 = send(other, to_sibling)
    far0 = send(near0, across)

    up, near1 = lax.optimization_barrier((up, near1))
    far_q0, far_q1, near_q1, up = call(
        up_kernel, "up", tables + [pair0, pair1, up], [sent, sent, sent, group], {6: 3}, scratch
    )
    part0 = send(far_q0, across)

    (here,) = call(
        group_kernel, "group", tables + [pair0, pair1, near0, near1, here], [group], {8: 0}, scratch
    )
    far0, far1, here, far_q1, near_q1 = lax.optimization_barrier(
        (far0, far1, here, far_q1, near_q1)
    )
    part1 = send(far_q1, lambda r, h, k: (r + 1, 1 - h, k))
    below1 = send(near_q1, lambda r, h, k: (r + 1, 1 - h, 1 - k))
    own_f1, other_q0, here = call(
        far_kernel, "far", tables + [far0, far1, here], [sums, sent, group], {6: 2}, scratch
    )
    here0 = send(other_q0, lambda r, h, k: (r, 1 - h, k))
    here_sib = send(own_f1, lambda r, h, k: (r, h, 1 - k))
    (below0,) = call(lambda *refs: add_kernel(2 * pb, *refs), "add_up", [up, part0], [sent])
    part1, _ = lax.optimization_barrier((part1, below0))
    (here1,) = call(lambda *refs: add_kernel(3 * pb, *refs), "add_here", [here, part1], [sent])
    below0 = send(below0, lambda r, h, k: (r + 1, 1 - h, k))
    here1 = send(here1, lambda r, h, k: (r, 1 - h, 1 - k))

    factor = jnp.broadcast_to(reflect[:, None], (piece_rows, half))
    args = [here, here_sib, here0, here1, below0, below1, source, factor]
    return pl.pallas_call(
        final_kernel,
        grid=(pb,),
        in_specs=[pl.BlockSpec(memory_space=pltpu.SMEM)]
        + [pl.BlockSpec(memory_space=pltpu.VMEM)] * len(args),
        out_specs=pl.BlockSpec((blk, width), lambda i: (i, 0)),
        out_shape=jax.ShapeDtypeStruct((piece_rows, width), f32),
        compiler_params=PARAMS,
        name="final",
    )(index, *map(in_vmem, args))


def solution(mesh):
    return jax.shard_map(
        per_device,
        mesh=mesh,
        in_specs=(
            P(("row", "col"), None),
            P(("row", "col"), None),
            P(("row", "col")),
            P(("row", "col"), None, None),
            P(("row", "col"), None),
            P(("row", "col"), None),
            P(("row", "col")),
        ),
        out_specs=P(("row", "col"), None),
        check_vma=False,
    )
```

```python
import jax
import jax.numpy as jnp
from jax import lax
from jax.experimental import pallas as pl
from jax.experimental.pallas import tpu as pltpu
from jax.sharding import PartitionSpec as P


AXES = ("row", "col")
SCALE_ROWS = 16
STEPS = 32766.0
LOG_STEPS = 256.0
LN2 = 0.6931471805599453
PARAMS = pltpu.CompilerParams(vmem_limit_bytes=12 * 1024 * 1024)


def send(x, route):
    groups, cols = lax.axis_size("row"), lax.axis_size("col")
    pairs = []
    for r in range(groups):
        for c in range(cols):
            to_r, to_h, to_k = route(r, c // 2, c % 2)
            if 0 <= to_r < groups:
                pairs.append((r * cols + c, to_r * cols + to_h * 2 + to_k))
    return lax.ppermute(x, AXES, pairs)


def quantized(x):
    top = jnp.max(jnp.abs(x), axis=0, keepdims=True)
    log = jnp.ceil(jnp.log(jnp.maximum(top, 1e-30)) * (LOG_STEPS / LN2))
    inverse = STEPS * jnp.exp(log * (-LN2 / LOG_STEPS))
    steps = jnp.round(x * inverse).astype(jnp.int32).astype(jnp.int16)
    return steps, log.astype(jnp.int32)


def store_quantized(ref, at, x):
    steps, log = quantized(x)
    blk, half = x.shape
    ref[at, :blk, :] = steps
    ref[at, blk:, :] = jnp.broadcast_to(log, (SCALE_ROWS, half)).astype(jnp.int16)


def load_quantized(ref, at, blk):
    log = ref[at, blk:, :].astype(jnp.int32).astype(jnp.float32)[:1]
    scale = jnp.exp(log * (LN2 / LOG_STEPS)) * (1.0 / STEPS)
    return ref[at, :blk, :].astype(jnp.int32).astype(jnp.float32) * scale


def split_columns(panel, k):
    half = panel.shape[1] // 2
    left, right = panel[:, :half], panel[:, half:]
    first = k == 0
    return jnp.where(first, left, right), jnp.where(first, right, left)


def goes_on(earlier, sums):
    pass


def products(mirror, direct, index, sib_index, blocks, sib_blocks, pieces, sums, plan, ring, x, sems):
    n_slots, blk = blocks.shape[0], blocks.shape[1]
    group = sums.shape[0]
    pb, depth = group // 4, ring.shape[0]
    turn = index[2 * n_slots + 1] * pb
    none = len(pieces)

    def planned(n, pick):
        def scan(is_sib, table):
            def step(slot, n):
                hit, piece, b, at = pick(table[slot] ^ turn, table[n_slots + slot] ^ turn)
                plan[n] = (((at * pb + b) * 8 + piece) * 2 + is_sib) * n_slots + slot
                return n + jnp.where(hit, 1, 0)

            return step

        end = lax.fori_loop(0, index[2 * n_slots], scan(0, index), n)
        end = lax.fori_loop(0, sib_index[2 * n_slots], scan(1, sib_index), end)

        @pl.when((end - n) % 2 == 1)
        def _():
            last = plan[end - 1]
            plan[end] = last + (none - last // (2 * n_slots) % 8) * (2 * n_slots)

        return end + (end - n) % 2

    def pick_mirror(row, col):
        hit, first = mirror(row // (2 * pb), col // group)
        return hit, first + row // pb % 2, row % pb, col % group

    def pick_direct(row, col):
        hit, first = direct(col // (2 * pb))
        return hit, first + col // pb % 2, col % pb, row

    zero = jnp.int32(0)
    n_mirror = planned(zero, pick_mirror) if mirror else zero
    n = planned(n_mirror, pick_direct) if direct else n_mirror

    def copy(source, slot, i):
        at = i % depth
        return pltpu.make_async_copy(source.at[slot], ring.at[at], sems.at[at])

    def start(i):
        @pl.when(i < n)
        def _():
            entry = plan[i]
            slot, is_sib = entry % n_slots, entry // n_slots % 2

            @pl.when(is_sib == 0)
            def _():
                copy(blocks, slot, i).start()

            @pl.when(is_sib == 1)
            def _():
                copy(sib_blocks, slot, i).start()

    for i in range(depth):
        start(i)

    def staged(i, u):
        entry = plan[i] // (2 * n_slots)
        piece, b, at = entry % 8, entry // 8 % pb, entry // (8 * pb)
        for p, ref in enumerate(pieces):

            @pl.when(piece == p)
            def _():
                x[u] = ref[pl.ds(pl.multiple_of(b * blk, blk), blk), :]

        @pl.when(piece == none)
        def _():
            x[u] = jnp.zeros(x.shape[1:], x.dtype)

        return at

    def steps(first, end, product):
        def step(pair, carry):
            i = first + 2 * pair
            places = [staged(i + u, u) for u in range(2)]
            for u in range(2):
                copy(blocks, 0, i + u).wait()
            results = [product(ring[(i + u) % depth], x[u]) for u in range(2)]
            for at, result in zip(places, results):
                sums[at] += result
            for u in range(2):
                start(i + u + depth)
            return carry

        lax.fori_loop(0, (end - first) // 2, step, 0)

    if mirror:
        steps(
            zero,
            n_mirror,
            lambda block, x: lax.dot_general(
                block, x, (((0,), (0,)), ((), ())), preferred_element_type=jnp.float32
            ),
        )
    if direct:
        steps(
            n_mirror, n, lambda block, x: jnp.dot(block, x, preferred_element_type=jnp.float32)
        )


def for_blocks(pb, body):
    def step(b, carry):
        body(b)
        return carry

    lax.fori_loop(0, pb, step, 0)


def to_next(pair):
    return lambda rows, ahead: ((rows == pair) & (ahead == 1), 0)


def to_own(pair):
    return lambda rows, ahead: ((rows == pair) & (ahead == 0), 0)


def from_pair(pair):
    return lambda cols: (cols == pair, 0)


def chip_up_kernel(*refs):
    tables, pieces, sums, scratch = refs[:4], refs[4:6], refs[6], refs[7:]
    sums[...] = jnp.zeros_like(sums)
    products(to_next(0), None, *tables, pieces, sums, *scratch)


def chip_here_kernel(*refs):
    tables, pieces, sums, scratch = refs[:4], refs[4:6], refs[6], refs[7:]
    sums[...] = jnp.zeros_like(sums)
    products(to_own(0), from_pair(0), *tables, pieces, sums, *scratch)


def up_kernel(*refs):
    tables, pieces, earlier = refs[:4], refs[4:6], refs[6]
    far0, far1, near1, sums = refs[7:11]
    goes_on(earlier, sums)
    products(to_next(1), None, *tables, pieces, sums, *refs[11:])
    pb = far0.shape[0]

    def finish(b):
        store_quantized(far1, b, sums[pb + b])
        store_quantized(far0, b, sums[b])
        store_quantized(near1, b, sums[3 * pb + b])

    for_blocks(pb, finish)


def group_kernel(*refs):
    tables, pieces, earlier, sums = refs[:4], refs[4:8], refs[8], refs[9]
    goes_on(earlier, sums)
    direct = lambda cols: ((cols == 1) | (cols == 3), jnp.where(cols == 3, 2, 0))
    products(to_own(1), direct, *tables, pieces, sums, *refs[10:])


def far_kernel(*refs):
    tables, pieces, earlier = refs[:4], refs[4:6], refs[6]
    own1, other0, sums = refs[7:10]
    goes_on(earlier, sums)
    products(None, from_pair(2), *tables, pieces, sums, *refs[10:])
    pb = own1.shape[0]

    def finish(b):
        store_quantized(other0, b, sums[2 * pb + b])
        own1[b] = sums[pb + b]

    for_blocks(pb, finish)


def add_kernel(first, sums, arrived, out):
    blk = sums.shape[1]

    def step(b):
        store_quantized(out, b, sums[first + b] + load_quantized(arrived, b, blk))

    for_blocks(out.shape[0], step)


def final_kernel(index, sums, sib, pair0, pair1, below0, below1, source, reflect, out):
    blk, half = sums.shape[1:]
    b = pl.program_id(0)
    mine = sums[b] + load_quantized(pair0, b, blk) + load_quantized(below0, b, blk)
    other = sib[b] + load_quantized(pair1, b, blk) + load_quantized(below1, b, blk)
    first = index[index.shape[0] - 1] % 2 == 0
    rows = pl.ds(pl.multiple_of(b * blk, blk), blk)
    factor = reflect[rows, :]
    left = jnp.where(first, mine, other)
    right = jnp.where(first, other, mine)
    out[:, :half] = source[rows, :half].astype(jnp.float32) + factor * left
    out[:, half:] = source[rows, half:].astype(jnp.float32) + factor * right


def in_vmem(x):
    return pltpu.with_memory_space_constraint(x, pltpu.VMEM)


def in_hbm(x):
    return pltpu.with_memory_space_constraint(x, pltpu.HBM)


def vmem_shape(shape, dtype):
    return pltpu.VMEM(shape, dtype)


def call(kernel, name, inputs, outputs, aliases=None, scratch=()):
    def spec(shape, dtype):
        if dtype == jnp.int32:
            return pl.BlockSpec(memory_space=pltpu.SMEM)
        if shape[-1] > 128 and len(shape) == 3:
            return pl.BlockSpec(memory_space=pltpu.HBM)
        return pl.BlockSpec(memory_space=pltpu.VMEM)

    specs = [spec(x.shape, x.dtype) for x in inputs]
    put = {pltpu.VMEM: in_vmem, pltpu.HBM: in_hbm, pltpu.SMEM: lambda x: x}
    return pl.pallas_call(
        kernel,
        in_specs=specs,
        out_specs=[pl.BlockSpec(memory_space=pltpu.VMEM)] * len(outputs),
        out_shape=[vmem_shape(*output) for output in outputs],
        scratch_shapes=scratch,
        input_output_aliases=aliases or {},
        compiler_params=PARAMS,
        cost_estimate=pl.CostEstimate(flops=1000, bytes_accessed=1000, transcendentals=0),
        name=name,
    )(*[put[s.memory_space](x) for x, s in zip(inputs, specs)])


def per_device(panel, source, reflect, blocks, blk_rows, blk_cols, live_count):
    f32 = jnp.float32
    piece_rows, width = panel.shape
    n_slots, blk, _ = blocks.shape
    half = width // 2
    pb = piece_rows // blk
    r, c = lax.axis_index("row"), lax.axis_index("col")
    k = c % 2

    base = r * (pb * lax.axis_size("col"))
    place = c.astype(jnp.int32)[None]
    index = jnp.concatenate([blk_rows[0] - base, blk_cols[0] - base, live_count, place])

    to_sibling = lambda r, h, k: (r, h, 1 - k)
    across = lambda r, h, k: (r, 1 - h, k)
    down = lambda r, h, k: (r - 1, 1 - h, k)
    pair = send(panel, across)
    near = send(panel, down)
    sib_blocks = send(blocks, to_sibling)
    mine, other = split_columns(panel, k)
    sib = send(other, to_sibling)
    sib_index = send(index, to_sibling)
    sums = ((pb, blk, half), f32)
    sent = ((pb, blk + SCALE_ROWS, half), jnp.int16)
    group = ((4 * pb, blk, half), f32)
    tables = [index, sib_index, blocks, sib_blocks]
    scratch = [
        pltpu.SMEM((4 * n_slots + 4,), jnp.int32),
        pltpu.VMEM((6, blk, blk), blocks.dtype),
        pltpu.VMEM((2, blk, half), panel.dtype),
        pltpu.SemaphoreType.DMA((6,)),
    ]

    (up,) = call(chip_up_kernel, "chip_up", tables + [mine, sib], [group], scratch=scratch)
    (here,) = call(chip_here_kernel, "chip_here", tables + [mine, sib], [group], scratch=scratch)
    pair, up, here = lax.optimization_barrier((pair, up, here))
    pair0, other = split_columns(pair, k)
    near, _ = lax.optimization_barrier((near, other))
    far1 = send(other, lambda r, h, k: (r - 1, 1 - h, 1 - k))
    pair1 = send(other, to_sibling)
    near0, other = split_columns(near, k)
    near1 = send(other, to_sibling)
    far0 = send(near0, across)

    up, near1 = lax.optimization_barrier((up, near1))
    far_q0, far_q1, near_q1, up = call(
        up_kernel, "up", tables + [pair0, pair1, up], [sent, sent, sent, group], {6: 3}, scratch
    )
    part0 = send(far_q0, across)

    (here,) = call(
        group_kernel, "group", tables + [pair0, pair1, near0, near1, here], [group], {8: 0}, scratch
    )
    here, far_q1 = lax.optimization_barrier((here, far_q1))
    part1 = send(far_q1, lambda r, h, k: (r + 1, 1 - h, k))
    far0, far1, here, near_q1 = lax.optimization_barrier((far0, far1, here, near_q1))
    below1 = send(near_q1, lambda r, h, k: (r + 1, 1 - h, 1 - k))
    own_f1, other_q0, here = call(
        far_kernel, "far", tables + [far0, far1, here], [sums, sent, group], {6: 2}, scratch
    )
    here0 = send(other_q0, lambda r, h, k: (r, 1 - h, k))
    here_sib = send(own_f1, lambda r, h, k: (r, h, 1 - k))
    (below0,) = call(lambda *refs: add_kernel(2 * pb, *refs), "add_up", [up, part0], [sent])
    part1, _ = lax.optimization_barrier((part1, below0))
    (here1,) = call(lambda *refs: add_kernel(3 * pb, *refs), "add_here", [here, part1], [sent])
    below0 = send(below0, lambda r, h, k: (r + 1, 1 - h, k))
    here1 = send(here1, lambda r, h, k: (r, 1 - h, 1 - k))

    factor = jnp.broadcast_to(reflect[:, None], (piece_rows, half))
    args = [here, here_sib, here0, here1, below0, below1, source, factor]
    return pl.pallas_call(
        final_kernel,
        grid=(pb,),
        in_specs=[pl.BlockSpec(memory_space=pltpu.SMEM)]
        + [pl.BlockSpec(memory_space=pltpu.VMEM)] * len(args),
        out_specs=pl.BlockSpec((blk, width), lambda i: (i, 0)),
        out_shape=jax.ShapeDtypeStruct((piece_rows, width), f32),
        compiler_params=PARAMS,
        name="final",
    )(index, *map(in_vmem, args))


def solution(mesh):
    return jax.shard_map(
        per_device,
        mesh=mesh,
        in_specs=(
            P(("row", "col"), None),
            P(("row", "col"), None),
            P(("row", "col")),
            P(("row", "col"), None, None),
            P(("row", "col"), None),
            P(("row", "col"), None),
            P(("row", "col")),
        ),
        out_specs=P(("row", "col"), None),
        check_vma=False,
    )
```

```python
import jax
import jax.numpy as jnp
from jax import lax
from jax.experimental import pallas as pl
from jax.experimental.pallas import tpu as pltpu
from jax.sharding import PartitionSpec as P


AXES = ("row", "col")
SCALE_ROWS = 16
STEPS = 32766.0
LOG_STEPS = 256.0
LN2 = 0.6931471805599453
PARAMS = pltpu.CompilerParams(vmem_limit_bytes=12 * 1024 * 1024)


def send(x, route):
    groups, cols = lax.axis_size("row"), lax.axis_size("col")
    pairs = []
    for r in range(groups):
        for c in range(cols):
            to_r, to_h, to_k = route(r, c // 2, c % 2)
            pairs.append((r * cols + c, to_r % groups * cols + to_h * 2 + to_k))
    return lax.ppermute(x, AXES, pairs)


def quantized(x):
    top = jnp.max(jnp.abs(x), axis=0, keepdims=True)
    log = jnp.ceil(jnp.log(jnp.maximum(top, 1e-30)) * (LOG_STEPS / LN2))
    inverse = STEPS * jnp.exp(log * (-LN2 / LOG_STEPS))
    steps = jnp.round(x * inverse).astype(jnp.int32).astype(jnp.int16)
    return steps, log.astype(jnp.int32)


def store_quantized(ref, at, x):
    steps, log = quantized(x)
    blk, half = x.shape
    ref[at, :blk, :] = steps
    ref[at, blk:, :] = jnp.broadcast_to(log, (SCALE_ROWS, half)).astype(jnp.int16)


def load_quantized(ref, at, blk):
    log = ref[at, blk:, :].astype(jnp.int32).astype(jnp.float32)[:1]
    scale = jnp.exp(log * (LN2 / LOG_STEPS)) * (1.0 / STEPS)
    return ref[at, :blk, :].astype(jnp.int32).astype(jnp.float32) * scale


def split_columns(panel, k):
    half = panel.shape[1] // 2
    left, right = panel[:, :half], panel[:, half:]
    first = k == 0
    return jnp.where(first, left, right), jnp.where(first, right, left)


def goes_on(earlier, sums):
    pass


def products(mirror, direct, index, sib_index, blocks, sib_blocks, pieces, sums, plan, ring, x, sems):
    n_slots, blk = blocks.shape[0], blocks.shape[1]
    group = sums.shape[0]
    pb, depth = group // 4, ring.shape[0]
    turn = index[2 * n_slots + 1] * pb
    none = len(pieces)

    def planned(n, pick):
        def scan(is_sib, table):
            def step(slot, n):
                hit, piece, b, at = pick(table[slot] ^ turn, table[n_slots + slot] ^ turn)
                plan[n] = (((at * pb + b) * 8 + piece) * 2 + is_sib) * n_slots + slot
                return n + jnp.where(hit, 1, 0)

            return step

        end = lax.fori_loop(0, index[2 * n_slots], scan(0, index), n)
        end = lax.fori_loop(0, sib_index[2 * n_slots], scan(1, sib_index), end)

        @pl.when((end - n) % 2 == 1)
        def _():
            last = plan[end - 1]
            plan[end] = last + (none - last // (2 * n_slots) % 8) * (2 * n_slots)

        return end + (end - n) % 2

    def pick_mirror(row, col):
        hit, first = mirror(row // (2 * pb), col // group)
        return hit, first + row // pb % 2, row % pb, col % group

    def pick_direct(row, col):
        hit, first = direct(col // (2 * pb))
        return hit, first + col // pb % 2, col % pb, row

    zero = jnp.int32(0)
    n_mirror = planned(zero, pick_mirror) if mirror else zero
    n = planned(n_mirror, pick_direct) if direct else n_mirror

    def copy(source, slot, i):
        at = i % depth
        return pltpu.make_async_copy(source.at[slot], ring.at[at], sems.at[at])

    def start(i):
        @pl.when(i < n)
        def _():
            entry = plan[i]
            slot, is_sib = entry % n_slots, entry // n_slots % 2

            @pl.when(is_sib == 0)
            def _():
                copy(blocks, slot, i).start()

            @pl.when(is_sib == 1)
            def _():
                copy(sib_blocks, slot, i).start()

    for i in range(depth):
        start(i)

    def staged(i, u):
        entry = plan[i] // (2 * n_slots)
        piece, b, at = entry % 8, entry // 8 % pb, entry // (8 * pb)
        for p, ref in enumerate(pieces):

            @pl.when(piece == p)
            def _():
                x[u] = ref[pl.ds(pl.multiple_of(b * blk, blk), blk), :]

        @pl.when(piece == none)
        def _():
            x[u] = jnp.zeros(x.shape[1:], x.dtype)

        return at

    def steps(first, end, product):
        def step(pair, carry):
            i = first + 2 * pair
            places = [staged(i + u, u) for u in range(2)]
            for u in range(2):
                copy(blocks, 0, i + u).wait()
            results = [product(ring[(i + u) % depth], x[u]) for u in range(2)]
            for at, result in zip(places, results):
                sums[at] += result
            for u in range(2):
                start(i + u + depth)
            return carry

        lax.fori_loop(0, (end - first) // 2, step, 0)

    if mirror:
        steps(
            zero,
            n_mirror,
            lambda block, x: lax.dot_general(
                block, x, (((0,), (0,)), ((), ())), preferred_element_type=jnp.float32
            ),
        )
    if direct:
        steps(
            n_mirror, n, lambda block, x: jnp.dot(block, x, preferred_element_type=jnp.float32)
        )


def for_blocks(pb, body):
    def step(b, carry):
        body(b)
        return carry

    lax.fori_loop(0, pb, step, 0)


def to_next(pair):
    return lambda rows, ahead: ((rows == pair) & (ahead == 1), 0)


def to_own(pair):
    return lambda rows, ahead: ((rows == pair) & (ahead == 0), 0)


def from_pair(pair):
    return lambda cols: (cols == pair, 0)


def chip_up_kernel(*refs):
    tables, pieces, sums, scratch = refs[:4], refs[4:6], refs[6], refs[7:]
    sums[...] = jnp.zeros_like(sums)
    products(to_next(0), None, *tables, pieces, sums, *scratch)


def chip_here_kernel(*refs):
    tables, pieces, sums, scratch = refs[:4], refs[4:6], refs[6], refs[7:]
    sums[...] = jnp.zeros_like(sums)
    products(to_own(0), from_pair(0), *tables, pieces, sums, *scratch)


def up_kernel(*refs):
    tables, pieces, earlier = refs[:4], refs[4:6], refs[6]
    far0, far1, sums = refs[7:10]
    goes_on(earlier, sums)
    products(to_next(1), None, *tables, pieces, sums, *refs[10:])
    n = far0.shape[0]
    for_blocks(n, lambda b: store_quantized(far0, b, sums[b]))
    for_blocks(far1.shape[0], lambda b: store_quantized(far1, b, sums[n + b]))


def group_kernel(*refs):
    tables, pieces, earlier, sums = refs[:4], refs[4:8], refs[8], refs[9]
    goes_on(earlier, sums)
    direct = lambda cols: ((cols == 1) | (cols == 3), jnp.where(cols == 3, 2, 0))
    products(to_own(1), direct, *tables, pieces, sums, *refs[10:])


def far_kernel(*refs):
    tables, pieces, earlier = refs[:4], refs[4:6], refs[6]
    own1, other0, sums = refs[7:10]
    goes_on(earlier, sums)
    products(None, from_pair(2), *tables, pieces, sums, *refs[10:])
    pb = own1.shape[0]

    def finish(b):
        store_quantized(other0, b, sums[2 * pb + b])
        store_quantized(own1, b, sums[pb + b])

    for_blocks(pb, finish)


def add_up_kernel(sums, arrived, out0, out1):
    pb, blk = out0.shape[0], sums.shape[1]
    for_blocks(
        pb, lambda b: store_quantized(out0, b, sums[2 * pb + b] + load_quantized(arrived, b, blk))
    )
    for_blocks(pb - 1, lambda b: store_quantized(out1, 1 + b, sums[3 * pb + 1 + b]))
    store_quantized(out1, 0, sums[3 * pb] + load_quantized(arrived, pb, blk))


def add_here_kernel(sums, arrived, out):
    pb, blk = out.shape[0], sums.shape[1]

    def step(b):
        store_quantized(out, 1 + b, sums[3 * pb + 1 + b] + load_quantized(arrived, b, blk))

    for_blocks(pb - 1, step)
    store_quantized(out, 0, sums[3 * pb])


def ready_kernel(index, sums, sib, here0, below1, source, reflect, mine, other):
    pb, blk, half = mine.shape
    first = index[index.shape[0] - 1] % 2 == 0

    def step(b):
        rows = pl.ds(pl.multiple_of(b * blk, blk), blk)
        factor = reflect[rows, :]
        left = source[rows, :half].astype(jnp.float32)
        right = source[rows, half:].astype(jnp.float32)
        add = factor * (sums[b] + load_quantized(here0, b, blk))
        mine[b] = jnp.where(first, left, right) + add
        add = factor * (load_quantized(sib, b, blk) + load_quantized(below1, b, blk))
        other[b] = jnp.where(first, right, left) + add

    for_blocks(pb, step)


def final_kernel(index, mine, other, below0, here1, reflect, out):
    blk, half = mine.shape[1:]
    b = pl.program_id(0)
    first = index[index.shape[0] - 1] % 2 == 0
    factor = reflect[pl.ds(pl.multiple_of(b * blk, blk), blk), :]
    a = mine[b] + factor * load_quantized(below0, b, blk)
    c = other[b] + factor * load_quantized(here1, b, blk)
    out[:, :half] = jnp.where(first, a, c)
    out[:, half:] = jnp.where(first, c, a)


def in_vmem(x):
    return pltpu.with_memory_space_constraint(x, pltpu.VMEM)


def in_hbm(x):
    return pltpu.with_memory_space_constraint(x, pltpu.HBM)


def vmem_shape(shape, dtype):
    return pltpu.VMEM(shape, dtype)


def call(kernel, name, inputs, outputs, aliases=None, scratch=()):
    def spec(shape, dtype):
        if dtype == jnp.int32:
            return pl.BlockSpec(memory_space=pltpu.SMEM)
        if shape[-1] > 128 and len(shape) == 3:
            return pl.BlockSpec(memory_space=pltpu.HBM)
        return pl.BlockSpec(memory_space=pltpu.VMEM)

    specs = [spec(x.shape, x.dtype) for x in inputs]
    put = {pltpu.VMEM: in_vmem, pltpu.HBM: in_hbm, pltpu.SMEM: lambda x: x}
    return pl.pallas_call(
        kernel,
        in_specs=specs,
        out_specs=[pl.BlockSpec(memory_space=pltpu.VMEM)] * len(outputs),
        out_shape=[vmem_shape(*output) for output in outputs],
        scratch_shapes=scratch,
        input_output_aliases=aliases or {},
        compiler_params=PARAMS,
        cost_estimate=pl.CostEstimate(flops=1000, bytes_accessed=1000, transcendentals=0),
        name=name,
    )(*[put[s.memory_space](x) for x, s in zip(inputs, specs)])


def per_device(panel, source, reflect, blocks, blk_rows, blk_cols, live_count):
    f32 = jnp.float32
    piece_rows, width = panel.shape
    n_slots, blk, _ = blocks.shape
    half = width // 2
    pb = piece_rows // blk
    r, c = lax.axis_index("row"), lax.axis_index("col")
    k = c % 2

    base = r * (pb * lax.axis_size("col"))
    place = c.astype(jnp.int32)[None]
    index = jnp.concatenate([blk_rows[0] - base, blk_cols[0] - base, live_count, place])

    to_sibling = lambda r, h, k: (r, h, 1 - k)
    across = lambda r, h, k: (r, 1 - h, k)
    down = lambda r, h, k: (r - 1, 1 - h, k)
    pair = send(panel, across)
    near = send(panel, down)
    sib_blocks = send(blocks, to_sibling)
    mine, other = split_columns(panel, k)
    sib = send(other, to_sibling)
    sib_index = send(index, to_sibling)
    sums = ((pb, blk, half), f32)
    sent = ((pb, blk + SCALE_ROWS, half), jnp.int16)
    group = ((4 * pb, blk, half), f32)
    tables = [index, sib_index, blocks, sib_blocks]
    scratch = [
        pltpu.SMEM((4 * n_slots + 4,), jnp.int32),
        pltpu.VMEM((6, blk, blk), blocks.dtype),
        pltpu.VMEM((2, blk, half), panel.dtype),
        pltpu.SemaphoreType.DMA((6,)),
    ]

    (up,) = call(chip_up_kernel, "chip_up", tables + [mine, sib], [group], scratch=scratch)
    (here,) = call(chip_here_kernel, "chip_here", tables + [mine, sib], [group], scratch=scratch)
    pair, up, here = lax.optimization_barrier((pair, up, here))
    pair0, other = split_columns(pair, k)
    near, _ = lax.optimization_barrier((near, other))
    far1 = send(other, lambda r, h, k: (r - 1, 1 - h, 1 - k))
    pair1 = send(other, to_sibling)
    near0, other = split_columns(near, k)
    near1 = send(other, to_sibling)
    far0 = send(near0, across)

    up, near1 = lax.optimization_barrier((up, near1))
    more, fewer = (((pb + n, *sent[0][1:]), sent[1]) for n in (1, -1))
    far_q0, far_q1, up = call(
        up_kernel, "up", tables + [pair0, pair1, up], [more, fewer, group], {6: 2}, scratch
    )
    part0 = send(far_q0, across)

    (here,) = call(
        group_kernel, "group", tables + [pair0, pair1, near0, near1, here], [group], {8: 0}, scratch
    )
    far0, far1, here, far_q1 = lax.optimization_barrier((far0, far1, here, far_q1))
    part1 = send(far_q1, lambda r, h, k: (r + 1, 1 - h, k))
    own_q1, other_q0, here = call(
        far_kernel, "far", tables + [far0, far1, here], [sent, sent, group], {6: 2}, scratch
    )
    here0 = send(other_q0, lambda r, h, k: (r, 1 - h, k))
    here_sib = send(own_q1, lambda r, h, k: (r, h, 1 - k))
    (here1,) = call(add_here_kernel, "add_here", [here, part1], [sent])
    part0, _ = lax.optimization_barrier((part0, here1))
    below0, below1 = call(add_up_kernel, "add_up", [up, part0], [sent, sent])
    below1 = send(below1, lambda r, h, k: (r + 1, 1 - h, 1 - k))
    below0 = send(below0, lambda r, h, k: (r + 1, 1 - h, k))
    here1 = send(here1, lambda r, h, k: (r, 1 - h, 1 - k))

    factor = jnp.broadcast_to(reflect[:, None], (piece_rows, half))
    ready = call(
        ready_kernel, "ready", [index, here, here_sib, here0, below1, source, factor], [sums, sums]
    )
    args = [*ready, below0, here1, factor]
    return pl.pallas_call(
        final_kernel,
        grid=(pb,),
        in_specs=[pl.BlockSpec(memory_space=pltpu.SMEM)]
        + [pl.BlockSpec(memory_space=pltpu.VMEM)] * len(args),
        out_specs=pl.BlockSpec((blk, width), lambda i: (i, 0)),
        out_shape=jax.ShapeDtypeStruct((piece_rows, width), f32),
        compiler_params=PARAMS,
        name="final",
    )(index, *map(in_vmem, args))


def solution(mesh):
    return jax.shard_map(
        per_device,
        mesh=mesh,
        in_specs=(
            P(("row", "col"), None),
            P(("row", "col"), None),
            P(("row", "col")),
            P(("row", "col"), None, None),
            P(("row", "col"), None),
            P(("row", "col"), None),
            P(("row", "col")),
        ),
        out_specs=P(("row", "col"), None),
        check_vma=False,
    )
```

```python
import jax
import jax.numpy as jnp
from jax import lax
from jax.experimental import pallas as pl
from jax.experimental.pallas import tpu as pltpu
from jax.sharding import PartitionSpec as P


AXES = ("row", "col")
SCALE_ROWS = 16
STEPS = 32766.0
LOG_STEPS = 256.0
LN2 = 0.6931471805599453
PARAMS = pltpu.CompilerParams(vmem_limit_bytes=12 * 1024 * 1024)


def send(x, route, wrap=True):
    groups, cols = lax.axis_size("row"), lax.axis_size("col")
    pairs = []
    for r in range(groups):
        for c in range(cols):
            to_r, to_h, to_k = route(r, c // 2, c % 2)
            if wrap or 0 <= to_r < groups:
                pairs.append((r * cols + c, to_r % groups * cols + to_h * 2 + to_k))
    return lax.ppermute(x, AXES, pairs)


def quantized(x):
    top = jnp.max(jnp.abs(x), axis=0, keepdims=True)
    log = jnp.ceil(jnp.log(jnp.maximum(top, 1e-30)) * (LOG_STEPS / LN2))
    inverse = STEPS * jnp.exp(log * (-LN2 / LOG_STEPS))
    steps = jnp.round(x * inverse).astype(jnp.int32).astype(jnp.int16)
    return steps, log.astype(jnp.int32)


def store_quantized(ref, at, x):
    steps, log = quantized(x)
    blk, half = x.shape
    ref[at, :blk, :] = steps
    ref[at, blk:, :] = jnp.broadcast_to(log, (SCALE_ROWS, half)).astype(jnp.int16)


def load_quantized(ref, at, blk):
    log = ref[at, blk:, :].astype(jnp.int32).astype(jnp.float32)[:1]
    scale = jnp.exp(log * (LN2 / LOG_STEPS)) * (1.0 / STEPS)
    return ref[at, :blk, :].astype(jnp.int32).astype(jnp.float32) * scale


def split_columns(panel, k):
    half = panel.shape[1] // 2
    left, right = panel[:, :half], panel[:, half:]
    first = k == 0
    return jnp.where(first, left, right), jnp.where(first, right, left)


def goes_on(earlier, sums):
    pass


def products(mirror, direct, index, sib_index, blocks, sib_blocks, pieces, sums, plan, ring, x, sems):
    n_slots, blk = blocks.shape[0], blocks.shape[1]
    group = sums.shape[0]
    pb, depth = group // 4, ring.shape[0]
    turn = index[2 * n_slots + 1] * pb
    none = len(pieces)

    def planned(n, pick):
        def scan(is_sib, table):
            def step(slot, n):
                hit, piece, b, at = pick(table[slot] ^ turn, table[n_slots + slot] ^ turn)
                plan[n] = (((at * pb + b) * 8 + piece) * 2 + is_sib) * n_slots + slot
                return n + jnp.where(hit, 1, 0)

            return step

        end = lax.fori_loop(0, index[2 * n_slots], scan(0, index), n)
        end = lax.fori_loop(0, sib_index[2 * n_slots], scan(1, sib_index), end)

        @pl.when((end - n) % 2 == 1)
        def _():
            last = plan[end - 1]
            plan[end] = last + (none - last // (2 * n_slots) % 8) * (2 * n_slots)

        return end + (end - n) % 2

    def pick_mirror(row, col):
        hit, first = mirror(row // (2 * pb), col // group)
        return hit, first + row // pb % 2, row % pb, col % group

    def pick_direct(row, col):
        hit, first = direct(col // (2 * pb))
        return hit, first + col // pb % 2, col % pb, row

    zero = jnp.int32(0)
    n_mirror = planned(zero, pick_mirror) if mirror else zero
    n = planned(n_mirror, pick_direct) if direct else n_mirror

    def copy(source, slot, i):
        at = i % depth
        return pltpu.make_async_copy(source.at[slot], ring.at[at], sems.at[at])

    def start(i):
        @pl.when(i < n)
        def _():
            entry = plan[i]
            slot, is_sib = entry % n_slots, entry // n_slots % 2

            @pl.when(is_sib == 0)
            def _():
                copy(blocks, slot, i).start()

            @pl.when(is_sib == 1)
            def _():
                copy(sib_blocks, slot, i).start()

    for i in range(depth):
        start(i)

    def staged(i, u):
        entry = plan[i] // (2 * n_slots)
        piece, b, at = entry % 8, entry // 8 % pb, entry // (8 * pb)
        for p, ref in enumerate(pieces):

            @pl.when(piece == p)
            def _():
                x[u] = ref[pl.ds(pl.multiple_of(b * blk, blk), blk), :]

        @pl.when(piece == none)
        def _():
            x[u] = jnp.zeros(x.shape[1:], x.dtype)

        return at

    def steps(first, end, product):
        def step(pair, carry):
            i = first + 2 * pair
            places = [staged(i + u, u) for u in range(2)]
            for u in range(2):
                copy(blocks, 0, i + u).wait()
            results = [product(ring[(i + u) % depth], x[u]) for u in range(2)]
            for at, result in zip(places, results):
                sums[at] += result
            for u in range(2):
                start(i + u + depth)
            return carry

        lax.fori_loop(0, (end - first) // 2, step, 0)

    if mirror:
        steps(
            zero,
            n_mirror,
            lambda block, x: lax.dot_general(
                block, x, (((0,), (0,)), ((), ())), preferred_element_type=jnp.float32
            ),
        )
    if direct:
        steps(
            n_mirror, n, lambda block, x: jnp.dot(block, x, preferred_element_type=jnp.float32)
        )


def for_blocks(pb, body):
    def step(b, carry):
        body(b)
        return carry

    lax.fori_loop(0, pb, step, 0)


def to_next(pair):
    return lambda rows, ahead: ((rows == pair) & (ahead == 1), 0)


def to_own(pair):
    return lambda rows, ahead: ((rows == pair) & (ahead == 0), 0)


def from_pair(pair):
    return lambda cols: (cols == pair, 0)


def chip_up_kernel(*refs):
    tables, pieces, sums, scratch = refs[:4], refs[4:6], refs[6], refs[7:]
    sums[...] = jnp.zeros_like(sums)
    products(to_next(0), None, *tables, pieces, sums, *scratch)


def chip_here_kernel(*refs):
    tables, pieces, sums, scratch = refs[:4], refs[4:6], refs[6], refs[7:]
    sums[...] = jnp.zeros_like(sums)
    products(to_own(0), from_pair(0), *tables, pieces, sums, *scratch)


def up_kernel(*refs):
    tables, pieces, earlier = refs[:4], refs[4:6], refs[6]
    far0, far1, near1, sums = refs[7:11]
    goes_on(earlier, sums)
    products(to_next(1), None, *tables, pieces, sums, *refs[11:])
    pb = far0.shape[0]

    def finish(b):
        store_quantized(far1, b, sums[pb + b])
        store_quantized(far0, b, sums[b])
        store_quantized(near1, b, sums[3 * pb + b])

    for_blocks(pb, finish)


def group_kernel(*refs):
    tables, pieces, earlier, sums = refs[:4], refs[4:8], refs[8], refs[9]
    goes_on(earlier, sums)
    direct = lambda cols: ((cols == 1) | (cols == 3), jnp.where(cols == 3, 2, 0))
    products(to_own(1), direct, *tables, pieces, sums, *refs[10:])


def far_kernel(*refs):
    tables, pieces, earlier = refs[:4], refs[4:6], refs[6]
    own1, other0, sums = refs[7:10]
    goes_on(earlier, sums)
    products(None, from_pair(2), *tables, pieces, sums, *refs[10:])
    pb = own1.shape[0]

    def finish(b):
        store_quantized(other0, b, sums[2 * pb + b])
        store_quantized(own1, b, sums[pb + b])

    for_blocks(pb, finish)


def add_kernel(first, sums, arrived, out):
    blk = sums.shape[1]

    def step(b):
        store_quantized(out, b, sums[first + b] + load_quantized(arrived, b, blk))

    for_blocks(out.shape[0], step)


def ready_kernel(index, sums, sib, here0, below1, source, reflect, mine, other):
    pb, blk, half = mine.shape
    first = index[index.shape[0] - 1] % 2 == 0

    def step(b):
        rows = pl.ds(pl.multiple_of(b * blk, blk), blk)
        factor = reflect[rows, :]
        left = source[rows, :half].astype(jnp.float32)
        right = source[rows, half:].astype(jnp.float32)
        add = factor * (sums[b] + load_quantized(here0, b, blk))
        mine[b] = jnp.where(first, left, right) + add
        add = factor * (load_quantized(sib, b, blk) + load_quantized(below1, b, blk))
        other[b] = jnp.where(first, right, left) + add

    for_blocks(pb, step)


def final_kernel(index, mine, other, below0, here1, reflect, out):
    blk, half = mine.shape[1:]
    b = pl.program_id(0)
    first = index[index.shape[0] - 1] % 2 == 0
    factor = reflect[pl.ds(pl.multiple_of(b * blk, blk), blk), :]
    a = mine[b] + factor * load_quantized(below0, b, blk)
    c = other[b] + factor * load_quantized(here1, b, blk)
    out[:, :half] = jnp.where(first, a, c)
    out[:, half:] = jnp.where(first, c, a)


def in_vmem(x):
    return pltpu.with_memory_space_constraint(x, pltpu.VMEM)


def in_hbm(x):
    return pltpu.with_memory_space_constraint(x, pltpu.HBM)


def vmem_shape(shape, dtype):
    return pltpu.VMEM(shape, dtype)


def call(kernel, name, inputs, outputs, aliases=None, scratch=()):
    def spec(shape, dtype):
        if dtype == jnp.int32:
            return pl.BlockSpec(memory_space=pltpu.SMEM)
        if shape[-1] > 128 and len(shape) == 3:
            return pl.BlockSpec(memory_space=pltpu.HBM)
        return pl.BlockSpec(memory_space=pltpu.VMEM)

    specs = [spec(x.shape, x.dtype) for x in inputs]
    put = {pltpu.VMEM: in_vmem, pltpu.HBM: in_hbm, pltpu.SMEM: lambda x: x}
    return pl.pallas_call(
        kernel,
        in_specs=specs,
        out_specs=[pl.BlockSpec(memory_space=pltpu.VMEM)] * len(outputs),
        out_shape=[vmem_shape(*output) for output in outputs],
        scratch_shapes=scratch,
        input_output_aliases=aliases or {},
        compiler_params=PARAMS,
        cost_estimate=pl.CostEstimate(flops=1000, bytes_accessed=1000, transcendentals=0),
        name=name,
    )(*[put[s.memory_space](x) for x, s in zip(inputs, specs)])


def per_device(panel, source, reflect, blocks, blk_rows, blk_cols, live_count):
    f32 = jnp.float32
    piece_rows, width = panel.shape
    n_slots, blk, _ = blocks.shape
    half = width // 2
    pb = piece_rows // blk
    r, c = lax.axis_index("row"), lax.axis_index("col")
    k = c % 2

    base = r * (pb * lax.axis_size("col"))
    place = c.astype(jnp.int32)[None]
    index = jnp.concatenate([blk_rows[0] - base, blk_cols[0] - base, live_count, place])

    to_sibling = lambda r, h, k: (r, h, 1 - k)
    across = lambda r, h, k: (r, 1 - h, k)
    down = lambda r, h, k: (r - 1, 1 - h, k)
    pair = send(panel, across)
    near = send(panel, down)
    sib_blocks = send(blocks, to_sibling)
    mine, other = split_columns(panel, k)
    sib = send(other, to_sibling)
    sib_index = send(index, to_sibling)
    sums = ((pb, blk, half), f32)
    sent = ((pb, blk + SCALE_ROWS, half), jnp.int16)
    group = ((4 * pb, blk, half), f32)
    tables = [index, sib_index, blocks, sib_blocks]
    scratch = [
        pltpu.SMEM((4 * n_slots + 4,), jnp.int32),
        pltpu.VMEM((6, blk, blk), blocks.dtype),
        pltpu.VMEM((2, blk, half), panel.dtype),
        pltpu.SemaphoreType.DMA((6,)),
    ]

    (up,) = call(chip_up_kernel, "chip_up", tables + [mine, sib], [group], scratch=scratch)
    (here,) = call(chip_here_kernel, "chip_here", tables + [mine, sib], [group], scratch=scratch)
    pair, up, here = lax.optimization_barrier((pair, up, here))
    pair0, other = split_columns(pair, k)
    near, _ = lax.optimization_barrier((near, other))
    far1 = send(other, lambda r, h, k: (r - 1, 1 - h, 1 - k))
    pair1 = send(other, to_sibling)
    near0, other = split_columns(near, k)
    near1 = send(other, to_sibling)
    far0 = send(near0, across)

    up, near1 = lax.optimization_barrier((up, near1))
    far_q0, far_q1, near_q1, up = call(
        up_kernel, "up", tables + [pair0, pair1, up], [sent, sent, sent, group], {6: 3}, scratch
    )
    part0 = send(far_q0, across)

    (here,) = call(
        group_kernel, "group", tables + [pair0, pair1, near0, near1, here], [group], {8: 0}, scratch
    )
    far0, far1, here, far_q1, near_q1 = lax.optimization_barrier(
        (far0, far1, here, far_q1, near_q1)
    )
    part1 = send(far_q1, lambda r, h, k: (r + 1, 1 - h, k))
    below1 = send(near_q1, lambda r, h, k: (r + 1, 1 - h, 1 - k), wrap=False)
    own_q1, other_q0, here = call(
        far_kernel, "far", tables + [far0, far1, here], [sent, sent, group], {6: 2}, scratch
    )
    here0 = send(other_q0, lambda r, h, k: (r, 1 - h, k))
    here_sib = send(own_q1, lambda r, h, k: (r, h, 1 - k))
    (below0,) = call(lambda *refs: add_kernel(2 * pb, *refs), "add_up", [up, part0], [sent])
    part1, _ = lax.optimization_barrier((part1, below0))
    (here1,) = call(lambda *refs: add_kernel(3 * pb, *refs), "add_here", [here, part1], [sent])
    below0 = send(below0, lambda r, h, k: (r + 1, 1 - h, k), wrap=False)
    here1 = send(here1, lambda r, h, k: (r, 1 - h, 1 - k))

    factor = jnp.broadcast_to(reflect[:, None], (piece_rows, half))
    ready = call(
        ready_kernel, "ready", [index, here, here_sib, here0, below1, source, factor], [sums, sums]
    )
    args = [*ready, below0, here1, factor]
    return pl.pallas_call(
        final_kernel,
        grid=(pb,),
        in_specs=[pl.BlockSpec(memory_space=pltpu.SMEM)]
        + [pl.BlockSpec(memory_space=pltpu.VMEM)] * len(args),
        out_specs=pl.BlockSpec((blk, width), lambda i: (i, 0)),
        out_shape=jax.ShapeDtypeStruct((piece_rows, width), f32),
        compiler_params=PARAMS,
        name="final",
    )(index, *map(in_vmem, args))


def solution(mesh):
    return jax.shard_map(
        per_device,
        mesh=mesh,
        in_specs=(
            P(("row", "col"), None),
            P(("row", "col"), None),
            P(("row", "col")),
            P(("row", "col"), None, None),
            P(("row", "col"), None),
            P(("row", "col"), None),
            P(("row", "col")),
        ),
        out_specs=P(("row", "col"), None),
        check_vma=False,
    )
```

```python
import jax
import jax.numpy as jnp
from jax import lax
from jax.experimental import pallas as pl
from jax.experimental.pallas import tpu as pltpu
from jax.sharding import PartitionSpec as P


AXES = ("row", "col")
SCALE_ROWS = 16
STEPS = 32766.0
LOG_STEPS = 256.0
LN2 = 0.6931471805599453
PARAMS = pltpu.CompilerParams(vmem_limit_bytes=12 * 1024 * 1024)


def send(x, route, wrap=True):
    groups, cols = lax.axis_size("row"), lax.axis_size("col")
    pairs = []
    for r in range(groups):
        for c in range(cols):
            to_r, to_h, to_k = route(r, c // 2, c % 2)
            if wrap or 0 <= to_r < groups:
                pairs.append((r * cols + c, to_r % groups * cols + to_h * 2 + to_k))
    return lax.ppermute(x, AXES, pairs)


def quantized(x):
    top = jnp.max(jnp.abs(x), axis=0, keepdims=True)
    log = jnp.ceil(jnp.log(jnp.maximum(top, 1e-30)) * (LOG_STEPS / LN2))
    inverse = STEPS * jnp.exp(log * (-LN2 / LOG_STEPS))
    steps = jnp.round(x * inverse).astype(jnp.int32).astype(jnp.int16)
    return steps, log.astype(jnp.int32)


def store_quantized(ref, at, x):
    steps, log = quantized(x)
    blk, half = x.shape
    ref[at, :blk, :] = steps
    ref[at, blk:, :] = jnp.broadcast_to(log, (SCALE_ROWS, half)).astype(jnp.int16)


def load_quantized(ref, at, blk):
    log = ref[at, blk:, :].astype(jnp.int32).astype(jnp.float32)[:1]
    scale = jnp.exp(log * (LN2 / LOG_STEPS)) * (1.0 / STEPS)
    return ref[at, :blk, :].astype(jnp.int32).astype(jnp.float32) * scale


def split_columns(panel, k):
    half = panel.shape[1] // 2
    left, right = panel[:, :half], panel[:, half:]
    first = k == 0
    return jnp.where(first, left, right), jnp.where(first, right, left)


def goes_on(earlier, sums):
    pass


def products(
    mirror, direct, index, sib_index, blocks, sib_blocks, pieces, sums, plan, ring, x, sems, moved=0
):
    n_slots, blk = blocks.shape[0], blocks.shape[1]
    group = sums.shape[0]
    pb, depth = group // 4, ring.shape[0]
    turn = index[2 * n_slots + 1] * pb
    none = len(pieces)

    def planned(n, pick):
        def scan(is_sib, table):
            def step(slot, n):
                hit, piece, b, at = pick(table[slot] ^ turn, table[n_slots + slot] ^ turn)
                plan[n] = (((at * 2 * pb + b) * 8 + piece) * 2 + is_sib) * n_slots + slot
                return n + jnp.where(hit, 1, 0)

            return step

        end = lax.fori_loop(0, index[2 * n_slots], scan(0, index), n)
        end = lax.fori_loop(0, sib_index[2 * n_slots], scan(1, sib_index), end)

        @pl.when((end - n) % 2 == 1)
        def _():
            last = plan[end - 1]
            plan[end] = last + (none - last // (2 * n_slots) % 8) * (2 * n_slots)

        return end + (end - n) % 2

    def pick_mirror(row, col):
        hit, first = mirror(row // (2 * pb), col // group)
        return hit, first + row // pb % 2, row % pb, col % group

    def pick_direct(row, col):
        hit, first = direct(col // (2 * pb))
        piece, b = first + col // pb % 2, col % pb
        if moved:
            b = col % (2 * pb)
            piece = jnp.where(b < pb + moved, 0, 1)
            b = b - piece * (pb + moved)
        return hit, piece, b, row

    zero = jnp.int32(0)
    n_mirror = planned(zero, pick_mirror) if mirror else zero
    n = planned(n_mirror, pick_direct) if direct else n_mirror

    def copy(source, slot, i):
        at = i % depth
        return pltpu.make_async_copy(source.at[slot], ring.at[at], sems.at[at])

    def start(i):
        @pl.when(i < n)
        def _():
            entry = plan[i]
            slot, is_sib = entry % n_slots, entry // n_slots % 2

            @pl.when(is_sib == 0)
            def _():
                copy(blocks, slot, i).start()

            @pl.when(is_sib == 1)
            def _():
                copy(sib_blocks, slot, i).start()

    for i in range(depth):
        start(i)

    def staged(i, u):
        entry = plan[i] // (2 * n_slots)
        piece, b, at = entry % 8, entry // 8 % (2 * pb), entry // (16 * pb)
        for p, ref in enumerate(pieces):

            @pl.when(piece == p)
            def _():
                x[u] = ref[pl.ds(pl.multiple_of(b * blk, blk), blk), :]

        @pl.when(piece == none)
        def _():
            x[u] = jnp.zeros(x.shape[1:], x.dtype)

        return at

    def steps(first, end, product):
        def step(pair, carry):
            i = first + 2 * pair
            places = [staged(i + u, u) for u in range(2)]
            for u in range(2):
                copy(blocks, 0, i + u).wait()
            results = [product(ring[(i + u) % depth], x[u]) for u in range(2)]
            for at, result in zip(places, results):
                sums[at] += result
            for u in range(2):
                start(i + u + depth)
            return carry

        lax.fori_loop(0, (end - first) // 2, step, 0)

    if mirror:
        steps(
            zero,
            n_mirror,
            lambda block, x: lax.dot_general(
                block, x, (((0,), (0,)), ((), ())), preferred_element_type=jnp.float32
            ),
        )
    if direct:
        steps(
            n_mirror, n, lambda block, x: jnp.dot(block, x, preferred_element_type=jnp.float32)
        )


def for_blocks(pb, body):
    def step(b, carry):
        body(b)
        return carry

    lax.fori_loop(0, pb, step, 0)


def to_next(pair):
    return lambda rows, ahead: ((rows == pair) & (ahead == 1), 0)


def to_own(pair):
    return lambda rows, ahead: ((rows == pair) & (ahead == 0), 0)


def from_pair(pair):
    return lambda cols: (cols == pair, 0)


def chip_up_kernel(*refs):
    tables, pieces, sums, scratch = refs[:4], refs[4:6], refs[6], refs[7:]
    sums[...] = jnp.zeros_like(sums)
    products(to_next(0), None, *tables, pieces, sums, *scratch)


def chip_here_kernel(*refs):
    tables, pieces, sums, scratch = refs[:4], refs[4:6], refs[6], refs[7:]
    sums[...] = jnp.zeros_like(sums)
    products(to_own(0), from_pair(0), *tables, pieces, sums, *scratch)


def up_kernel(*refs):
    tables, pieces, earlier = refs[:4], refs[4:6], refs[6]
    far0, far1, near1, sums = refs[7:11]
    goes_on(earlier, sums)
    products(to_next(1), None, *tables, pieces, sums, *refs[11:])
    pb = far0.shape[0]

    def finish(b):
        store_quantized(far1, b, sums[pb + b])
        store_quantized(far0, b, sums[b])
        store_quantized(near1, b, sums[3 * pb + b])

    for_blocks(pb, finish)


def group_kernel(*refs):
    tables, pieces, earlier, sums = refs[:4], refs[4:8], refs[8], refs[9]
    goes_on(earlier, sums)
    direct = lambda cols: ((cols == 1) | (cols == 3), jnp.where(cols == 3, 2, 0))
    products(to_own(1), direct, *tables, pieces, sums, *refs[10:])


def far_kernel(*refs):
    tables, pieces, earlier = refs[:4], refs[4:6], refs[6]
    own1, other0, sums = refs[7:10]
    goes_on(earlier, sums)
    products(None, from_pair(2), *tables, pieces, sums, *refs[10:], moved=1)
    pb = own1.shape[0]

    def finish(b):
        store_quantized(other0, b, sums[2 * pb + b])
        store_quantized(own1, b, sums[pb + b])

    for_blocks(pb, finish)


def add_kernel(first, sums, arrived, out):
    blk = sums.shape[1]

    def step(b):
        store_quantized(out, b, sums[first + b] + load_quantized(arrived, b, blk))

    for_blocks(out.shape[0], step)


def ready_kernel(index, sums, sib, here0, below1, source, reflect, mine, other):
    pb, blk, half = mine.shape
    first = index[index.shape[0] - 1] % 2 == 0

    def step(b):
        rows = pl.ds(pl.multiple_of(b * blk, blk), blk)
        factor = reflect[rows, :]
        left = source[rows, :half].astype(jnp.float32)
        right = source[rows, half:].astype(jnp.float32)
        add = factor * (sums[b] + load_quantized(here0, b, blk))
        mine[b] = jnp.where(first, left, right) + add
        add = factor * (load_quantized(sib, b, blk) + load_quantized(below1, b, blk))
        other[b] = jnp.where(first, right, left) + add

    for_blocks(pb, step)


def final_kernel(index, mine, other, below0, here1, reflect, out):
    blk, half = mine.shape[1:]
    b = pl.program_id(0)
    first = index[index.shape[0] - 1] % 2 == 0
    factor = reflect[pl.ds(pl.multiple_of(b * blk, blk), blk), :]
    a = mine[b] + factor * load_quantized(below0, b, blk)
    c = other[b] + factor * load_quantized(here1, b, blk)
    out[:, :half] = jnp.where(first, a, c)
    out[:, half:] = jnp.where(first, c, a)


def in_vmem(x):
    return pltpu.with_memory_space_constraint(x, pltpu.VMEM)


def in_hbm(x):
    return pltpu.with_memory_space_constraint(x, pltpu.HBM)


def vmem_shape(shape, dtype):
    return pltpu.VMEM(shape, dtype)


def call(kernel, name, inputs, outputs, aliases=None, scratch=()):
    def spec(shape, dtype):
        if dtype == jnp.int32:
            return pl.BlockSpec(memory_space=pltpu.SMEM)
        if shape[-1] > 128 and len(shape) == 3:
            return pl.BlockSpec(memory_space=pltpu.HBM)
        return pl.BlockSpec(memory_space=pltpu.VMEM)

    specs = [spec(x.shape, x.dtype) for x in inputs]
    put = {pltpu.VMEM: in_vmem, pltpu.HBM: in_hbm, pltpu.SMEM: lambda x: x}
    return pl.pallas_call(
        kernel,
        in_specs=specs,
        out_specs=[pl.BlockSpec(memory_space=pltpu.VMEM)] * len(outputs),
        out_shape=[vmem_shape(*output) for output in outputs],
        scratch_shapes=scratch,
        input_output_aliases=aliases or {},
        compiler_params=PARAMS,
        cost_estimate=pl.CostEstimate(flops=1000, bytes_accessed=1000, transcendentals=0),
        name=name,
    )(*[put[s.memory_space](x) for x, s in zip(inputs, specs)])


def per_device(panel, source, reflect, blocks, blk_rows, blk_cols, live_count):
    f32 = jnp.float32
    piece_rows, width = panel.shape
    n_slots, blk, _ = blocks.shape
    half = width // 2
    pb = piece_rows // blk
    r, c = lax.axis_index("row"), lax.axis_index("col")
    k = c % 2

    base = r * (pb * lax.axis_size("col"))
    place = c.astype(jnp.int32)[None]
    index = jnp.concatenate([blk_rows[0] - base, blk_cols[0] - base, live_count, place])

    to_sibling = lambda r, h, k: (r, h, 1 - k)
    across = lambda r, h, k: (r, 1 - h, k)
    down = lambda r, h, k: (r - 1, 1 - h, k)
    pair = send(panel, across)
    near = send(panel, down)
    sib_blocks = send(blocks, to_sibling)
    mine, other = split_columns(panel, k)
    sib = send(other, to_sibling)
    sib_index = send(index, to_sibling)
    sums = ((pb, blk, half), f32)
    sent = ((pb, blk + SCALE_ROWS, half), jnp.int16)
    group = ((4 * pb, blk, half), f32)
    tables = [index, sib_index, blocks, sib_blocks]
    scratch = [
        pltpu.SMEM((4 * n_slots + 4,), jnp.int32),
        pltpu.VMEM((6, blk, blk), blocks.dtype),
        pltpu.VMEM((2, blk, half), panel.dtype),
        pltpu.SemaphoreType.DMA((6,)),
    ]

    (up,) = call(chip_up_kernel, "chip_up", tables + [mine, sib], [group], scratch=scratch)
    (here,) = call(chip_here_kernel, "chip_here", tables + [mine, sib], [group], scratch=scratch)
    pair, up, here = lax.optimization_barrier((pair, up, here))
    pair0, other = split_columns(pair, k)
    near, _ = lax.optimization_barrier((near, other))
    far1 = send(other[blk:], lambda r, h, k: (r - 1, 1 - h, 1 - k))
    pair1 = send(other, to_sibling)
    near0, other = split_columns(near, k)
    near1 = send(other, to_sibling)
    far0 = send(jnp.concatenate([near0, near1[:blk]]), across)

    up, near1 = lax.optimization_barrier((up, near1))
    far_q0, far_q1, near_q1, up = call(
        up_kernel, "up", tables + [pair0, pair1, up], [sent, sent, sent, group], {6: 3}, scratch
    )
    part0 = send(far_q0, across)

    (here,) = call(
        group_kernel, "group", tables + [pair0, pair1, near0, near1, here], [group], {8: 0}, scratch
    )
    far1, here, far_q1, near_q1 = lax.optimization_barrier((far1, here, far_q1, near_q1))
    far0, near_q1 = lax.optimization_barrier((far0, near_q1))
    part1 = send(far_q1, lambda r, h, k: (r + 1, 1 - h, k))
    below1 = send(near_q1, lambda r, h, k: (r + 1, 1 - h, 1 - k), wrap=False)
    own_q1, other_q0, here = call(
        far_kernel, "far", tables + [far0, far1, here], [sent, sent, group], {6: 2}, scratch
    )
    here0 = send(other_q0, lambda r, h, k: (r, 1 - h, k))
    here_sib = send(own_q1, lambda r, h, k: (r, h, 1 - k))
    part0, _ = lax.optimization_barrier((part0, other_q0))
    (below0,) = call(lambda *refs: add_kernel(2 * pb, *refs), "add_up", [up, part0], [sent])
    part1, _ = lax.optimization_barrier((part1, below0))
    (here1,) = call(lambda *refs: add_kernel(3 * pb, *refs), "add_here", [here, part1], [sent])
    below0 = send(below0, lambda r, h, k: (r + 1, 1 - h, k), wrap=False)
    here1 = send(here1, lambda r, h, k: (r, 1 - h, 1 - k))

    factor = jnp.broadcast_to(reflect[:, None], (piece_rows, half))
    ready = call(
        ready_kernel, "ready", [index, here, here_sib, here0, below1, source, factor], [sums, sums]
    )
    args = [*ready, below0, here1, factor]
    return pl.pallas_call(
        final_kernel,
        grid=(pb,),
        in_specs=[pl.BlockSpec(memory_space=pltpu.SMEM)]
        + [pl.BlockSpec(memory_space=pltpu.VMEM)] * len(args),
        out_specs=pl.BlockSpec((blk, width), lambda i: (i, 0)),
        out_shape=jax.ShapeDtypeStruct((piece_rows, width), f32),
        compiler_params=PARAMS,
        name="final",
    )(index, *map(in_vmem, args))


def solution(mesh):
    return jax.shard_map(
        per_device,
        mesh=mesh,
        in_specs=(
            P(("row", "col"), None),
            P(("row", "col"), None),
            P(("row", "col")),
            P(("row", "col"), None, None),
            P(("row", "col"), None),
            P(("row", "col"), None),
            P(("row", "col")),
        ),
        out_specs=P(("row", "col"), None),
        check_vma=False,
    )
```

```python
import jax
import jax.numpy as jnp
from jax import lax
from jax.experimental import pallas as pl
from jax.experimental.pallas import tpu as pltpu
from jax.sharding import PartitionSpec as P


AXES = ("row", "col")
SCALE_ROWS = 16
STEPS = 32766.0
LOG_STEPS = 256.0
LN2 = 0.6931471805599453
PARAMS = pltpu.CompilerParams(vmem_limit_bytes=12 * 1024 * 1024)


def send(x, route, wrap=True):
    groups, cols = lax.axis_size("row"), lax.axis_size("col")
    pairs = []
    for r in range(groups):
        for c in range(cols):
            to_r, to_h, to_k = route(r, c // 2, c % 2)
            if wrap or 0 <= to_r < groups:
                pairs.append((r * cols + c, to_r % groups * cols + to_h * 2 + to_k))
    return lax.ppermute(x, AXES, pairs)


def quantized(x):
    top = jnp.max(jnp.abs(x), axis=0, keepdims=True)
    log = jnp.ceil(jnp.log(jnp.maximum(top, 1e-30)) * (LOG_STEPS / LN2))
    inverse = STEPS * jnp.exp(log * (-LN2 / LOG_STEPS))
    steps = jnp.round(x * inverse).astype(jnp.int32).astype(jnp.int16)
    return steps, log.astype(jnp.int32)


def store_quantized(ref, at, x):
    steps, log = quantized(x)
    blk, half = x.shape
    ref[at, :blk, :] = steps
    ref[at, blk:, :] = jnp.broadcast_to(log, (SCALE_ROWS, half)).astype(jnp.int16)


def load_quantized(ref, at, blk):
    log = ref[at, blk:, :].astype(jnp.int32).astype(jnp.float32)[:1]
    scale = jnp.exp(log * (LN2 / LOG_STEPS)) * (1.0 / STEPS)
    return ref[at, :blk, :].astype(jnp.int32).astype(jnp.float32) * scale


def split_columns(panel, k):
    half = panel.shape[1] // 2
    left, right = panel[:, :half], panel[:, half:]
    first = k == 0
    return jnp.where(first, left, right), jnp.where(first, right, left)


def goes_on(earlier, sums):
    pass


def products(mirror, direct, index, sib_index, blocks, sib_blocks, pieces, sums, plan, ring, x, sems):
    n_slots, blk = blocks.shape[0], blocks.shape[1]
    group = sums.shape[0]
    pb, depth = group // 4, ring.shape[0]
    turn = index[2 * n_slots + 1] * pb
    none = len(pieces)

    def planned(n, pick):
        def scan(is_sib, table):
            def step(slot, n):
                hit, piece, b, at = pick(table[slot] ^ turn, table[n_slots + slot] ^ turn)
                plan[n] = (((at * pb + b) * 8 + piece) * 2 + is_sib) * n_slots + slot
                return n + jnp.where(hit, 1, 0)

            return step

        end = lax.fori_loop(0, index[2 * n_slots], scan(0, index), n)
        end = lax.fori_loop(0, sib_index[2 * n_slots], scan(1, sib_index), end)

        @pl.when((end - n) % 2 == 1)
        def _():
            last = plan[end - 1]
            plan[end] = last + (none - last // (2 * n_slots) % 8) * (2 * n_slots)

        return end + (end - n) % 2

    def pick_mirror(row, col):
        hit, first = mirror(row // (2 * pb), col // group)
        return hit, first + row // pb % 2, row % pb, col % group

    def pick_direct(row, col):
        hit, first = direct(col // (2 * pb))
        return hit, first + col // pb % 2, col % pb, row

    zero = jnp.int32(0)
    n_mirror = planned(zero, pick_mirror) if mirror else zero
    n = planned(n_mirror, pick_direct) if direct else n_mirror

    def copy(source, slot, i):
        at = i % depth
        return pltpu.make_async_copy(source.at[slot], ring.at[at], sems.at[at])

    def start(i):
        @pl.when(i < n)
        def _():
            entry = plan[i]
            slot, is_sib = entry % n_slots, entry // n_slots % 2

            @pl.when(is_sib == 0)
            def _():
                copy(blocks, slot, i).start()

            @pl.when(is_sib == 1)
            def _():
                copy(sib_blocks, slot, i).start()

    for i in range(depth):
        start(i)

    def staged(i, u):
        entry = plan[i] // (2 * n_slots)
        piece, b, at = entry % 8, entry // 8 % pb, entry // (8 * pb)
        for p, ref in enumerate(pieces):

            @pl.when(piece == p)
            def _():
                x[u] = ref[pl.ds(pl.multiple_of(b * blk, blk), blk), :]

        @pl.when(piece == none)
        def _():
            x[u] = jnp.zeros(x.shape[1:], x.dtype)

        return at

    def steps(first, end, product):
        def step(pair, carry):
            i = first + 2 * pair
            places = [staged(i + u, u) for u in range(2)]
            for u in range(2):
                copy(blocks, 0, i + u).wait()
            results = [product(ring[(i + u) % depth], x[u]) for u in range(2)]
            for at, result in zip(places, results):
                sums[at] += result
            for u in range(2):
                start(i + u + depth)
            return carry

        lax.fori_loop(0, (end - first) // 2, step, 0)

    if mirror:
        steps(
            zero,
            n_mirror,
            lambda block, x: lax.dot_general(
                block, x, (((0,), (0,)), ((), ())), preferred_element_type=jnp.float32
            ),
        )
    if direct:
        steps(
            n_mirror, n, lambda block, x: jnp.dot(block, x, preferred_element_type=jnp.float32)
        )


def for_blocks(pb, body):
    def step(b, carry):
        body(b)
        return carry

    lax.fori_loop(0, pb, step, 0)


def to_next(pair):
    return lambda rows, ahead: ((rows == pair) & (ahead == 1), 0)


def to_own(pair):
    return lambda rows, ahead: ((rows == pair) & (ahead == 0), 0)


def from_pair(pair):
    return lambda cols: (cols == pair, 0)


def chip_up_kernel(*refs):
    tables, pieces, sums, scratch = refs[:4], refs[4:6], refs[6], refs[7:]
    sums[...] = jnp.zeros_like(sums)
    products(to_next(0), None, *tables, pieces, sums, *scratch)


def chip_here_kernel(*refs):
    tables, pieces, sums, scratch = refs[:4], refs[4:6], refs[6], refs[7:]
    sums[...] = jnp.zeros_like(sums)
    products(to_own(0), from_pair(0), *tables, pieces, sums, *scratch)


def up_kernel(*refs):
    tables, pieces, earlier = refs[:4], refs[4:6], refs[6]
    far0, far1, near1, sums = refs[7:11]
    goes_on(earlier, sums)
    products(to_next(1), None, *tables, pieces, sums, *refs[11:])
    pb = far0.shape[0]

    def finish(b):
        store_quantized(far1, b, sums[pb + b])
        store_quantized(far0, b, sums[b])
        store_quantized(near1, b, sums[3 * pb + b])

    for_blocks(pb, finish)


def group_kernel(*refs):
    tables, pieces, earlier, sums = refs[:4], refs[4:8], refs[8], refs[9]
    goes_on(earlier, sums)
    direct = lambda cols: ((cols == 1) | (cols == 3), jnp.where(cols == 3, 2, 0))
    products(to_own(1), direct, *tables, pieces, sums, *refs[10:])


def far_kernel(*refs):
    tables, pieces, earlier = refs[:4], refs[4:6], refs[6]
    own1, other0, sums = refs[7:10]
    goes_on(earlier, sums)
    products(None, from_pair(2), *tables, pieces, sums, *refs[10:])
    pb = own1.shape[0]

    def finish(b):
        store_quantized(other0, b, sums[2 * pb + b])
        store_quantized(own1, b, sums[pb + b])

    for_blocks(pb, finish)


def add_kernel(first, sums, arrived, out):
    blk = sums.shape[1]

    def step(b):
        store_quantized(out, b, sums[first + b] + load_quantized(arrived, b, blk))

    for_blocks(out.shape[0], step)


def ready_kernel(index, sums, sib, here0, below1, source, reflect, mine, other):
    pb, blk, half = mine.shape
    first = index[index.shape[0] - 1] % 2 == 0

    def step(b):
        rows = pl.ds(pl.multiple_of(b * blk, blk), blk)
        factor = reflect[rows, :]
        left = source[rows, :half].astype(jnp.float32)
        right = source[rows, half:].astype(jnp.float32)
        add = factor * (sums[b] + load_quantized(here0, b, blk))
        mine[b] = jnp.where(first, left, right) + add
        add = factor * (load_quantized(sib, b, blk) + load_quantized(below1, b, blk))
        other[b] = jnp.where(first, right, left) + add

    for_blocks(pb, step)


def final_kernel(index, mine, other, below0, here1, reflect, out):
    blk, half = mine.shape[1:]
    b = pl.program_id(0)
    first = index[index.shape[0] - 1] % 2 == 0
    factor = reflect[pl.ds(pl.multiple_of(b * blk, blk), blk), :]
    a = mine[b] + factor * load_quantized(below0, b, blk)
    c = other[b] + factor * load_quantized(here1, b, blk)
    out[:, :half] = jnp.where(first, a, c)
    out[:, half:] = jnp.where(first, c, a)


def in_vmem(x):
    return pltpu.with_memory_space_constraint(x, pltpu.VMEM)


def in_hbm(x):
    return pltpu.with_memory_space_constraint(x, pltpu.HBM)


def vmem_shape(shape, dtype):
    return pltpu.VMEM(shape, dtype)


def call(kernel, name, inputs, outputs, aliases=None, scratch=()):
    def spec(shape, dtype):
        if dtype == jnp.int32:
            return pl.BlockSpec(memory_space=pltpu.SMEM)
        if shape[-1] > 128 and len(shape) == 3:
            return pl.BlockSpec(memory_space=pltpu.HBM)
        return pl.BlockSpec(memory_space=pltpu.VMEM)

    specs = [spec(x.shape, x.dtype) for x in inputs]
    put = {pltpu.VMEM: in_vmem, pltpu.HBM: in_hbm, pltpu.SMEM: lambda x: x}
    return pl.pallas_call(
        kernel,
        in_specs=specs,
        out_specs=[pl.BlockSpec(memory_space=pltpu.VMEM)] * len(outputs),
        out_shape=[vmem_shape(*output) for output in outputs],
        scratch_shapes=scratch,
        input_output_aliases=aliases or {},
        compiler_params=PARAMS,
        cost_estimate=pl.CostEstimate(flops=1000, bytes_accessed=1000, transcendentals=0),
        name=name,
    )(*[put[s.memory_space](x) for x, s in zip(inputs, specs)])


def per_device(panel, source, reflect, blocks, blk_rows, blk_cols, live_count):
    f32 = jnp.float32
    piece_rows, width = panel.shape
    n_slots, blk, _ = blocks.shape
    half = width // 2
    pb = piece_rows // blk
    r, c = lax.axis_index("row"), lax.axis_index("col")
    k = c % 2

    base = r * (pb * lax.axis_size("col"))
    place = c.astype(jnp.int32)[None]
    index = jnp.concatenate([blk_rows[0] - base, blk_cols[0] - base, live_count, place])

    to_sibling = lambda r, h, k: (r, h, 1 - k)
    across = lambda r, h, k: (r, 1 - h, k)
    down = lambda r, h, k: (r - 1, 1 - h, k)
    pair = send(panel, across)
    near = send(panel, down)
    sib_blocks = send(blocks, to_sibling)
    mine, other = split_columns(panel, k)
    sib = send(other, to_sibling)
    sib_index = send(index, to_sibling)
    sums = ((pb, blk, half), f32)
    sent = ((pb, blk + SCALE_ROWS, half), jnp.int16)
    group = ((4 * pb, blk, half), f32)
    tables = [index, sib_index, blocks, sib_blocks]
    scratch = [
        pltpu.SMEM((4 * n_slots + 4,), jnp.int32),
        pltpu.VMEM((6, blk, blk), blocks.dtype),
        pltpu.VMEM((2, blk, half), panel.dtype),
        pltpu.SemaphoreType.DMA((6,)),
    ]

    (up,) = call(chip_up_kernel, "chip_up", tables + [mine, sib], [group], scratch=scratch)
    (here,) = call(chip_here_kernel, "chip_here", tables + [mine, sib], [group], scratch=scratch)
    pair, up, here = lax.optimization_barrier((pair, up, here))
    pair0, other = split_columns(pair, k)
    near, _ = lax.optimization_barrier((near, other))
    far1 = send(other, lambda r, h, k: (r - 1, 1 - h, 1 - k), wrap=False)
    pair1 = send(other, to_sibling)
    near0, other = split_columns(near, k)
    near1 = send(other, to_sibling)
    far0 = send(near0, across)

    up, near1 = lax.optimization_barrier((up, near1))
    far_q0, far_q1, near_q1, up = call(
        up_kernel, "up", tables + [pair0, pair1, up], [sent, sent, sent, group], {6: 3}, scratch
    )
    part0 = send(far_q0, across)

    (here,) = call(
        group_kernel, "group", tables + [pair0, pair1, near0, near1, here], [group], {8: 0}, scratch
    )
    far0, far1, here, far_q1, near_q1 = lax.optimization_barrier(
        (far0, far1, here, far_q1, near_q1)
    )
    part1 = send(far_q1, lambda r, h, k: (r + 1, 1 - h, k))
    below1 = send(near_q1, lambda r, h, k: (r + 1, 1 - h, 1 - k), wrap=False)
    own_q1, other_q0, here = call(
        far_kernel, "far", tables + [far0, far1, here], [sent, sent, group], {6: 2}, scratch
    )
    here0 = send(other_q0, lambda r, h, k: (r, 1 - h, k))
    here_sib = send(own_q1, lambda r, h, k: (r, h, 1 - k))
    (below0,) = call(lambda *refs: add_kernel(2 * pb, *refs), "add_up", [up, part0], [sent])
    part1, _ = lax.optimization_barrier((part1, below0))
    (here1,) = call(lambda *refs: add_kernel(3 * pb, *refs), "add_here", [here, part1], [sent])
    below0 = send(below0, lambda r, h, k: (r + 1, 1 - h, k), wrap=False)
    here1 = send(here1, lambda r, h, k: (r, 1 - h, 1 - k))

    factor = jnp.broadcast_to(reflect[:, None], (piece_rows, half))
    ready = call(
        ready_kernel, "ready", [index, here, here_sib, here0, below1, source, factor], [sums, sums]
    )
    args = [*ready, below0, here1, factor]
    return pl.pallas_call(
        final_kernel,
        grid=(pb,),
        in_specs=[pl.BlockSpec(memory_space=pltpu.SMEM)]
        + [pl.BlockSpec(memory_space=pltpu.VMEM)] * len(args),
        out_specs=pl.BlockSpec((blk, width), lambda i: (i, 0)),
        out_shape=jax.ShapeDtypeStruct((piece_rows, width), f32),
        compiler_params=PARAMS,
        name="final",
    )(index, *map(in_vmem, args))


def solution(mesh):
    return jax.shard_map(
        per_device,
        mesh=mesh,
        in_specs=(
            P(("row", "col"), None),
            P(("row", "col"), None),
            P(("row", "col")),
            P(("row", "col"), None, None),
            P(("row", "col"), None),
            P(("row", "col"), None),
            P(("row", "col")),
        ),
        out_specs=P(("row", "col"), None),
        check_vma=False,
    )
```
